32 devices in a mesh: groups: 2 (over y), inst: 4 (over z), mp: 4 (over x, core).
Axes of the slice: x: 2, y: 2, z: 4, core: 2. Of those that a mesh axis runs over, the one named last changes fastest.
Arguments:
- hidden_states: bfloat16 [3, 64, 5120], P(None, ('groups', 'inst'), 'mp'), parts along dimension 1, may hold values from -6 to 6
- kv_weight: bfloat16 [5120, 1024], P('mp'), may hold values from -0.078125 to 0.078125
- key_gain: float32 [128], replicated, may hold values from 0.1 to 1.9
- queries: bfloat16 [3, 64, 4096], P(None, ('groups', 'inst')), parts along dimension 1, may hold values from -128 to 128
- kv_pool: bfloat16 [8, 40, 16, 1024], P(('groups', 'inst'), 'mp'), parts along dimension 0, may hold values from -6 to 6
- page_table: int32 [64, 1, 4], P(('groups', 'inst'), None, 'mp'), parts along dimension 0, may hold values from 0 to 9, as said below
- lengths: int32 [64], P(('groups', 'inst')), parts along dimension 0, may hold values from 1 to 61, 976 in all
- mig_dest: int32 [8, 2], P('groups'), parts along dimension 0, may hold values from 0 to 3, as said below
- mig_local: int32 [8, 2], P('groups'), parts along dimension 0, may hold values from 0 to 7, as said below
- mig_slots: int32 [8, 2, 1, 4], P(('groups', 'inst'), None, None, 'mp'), parts along dimension 0, may hold values from 0 to 9, as said below
Outputs:
- attended: bfloat16 [3, 64, 4096], P(None, ('groups', 'inst'), 'mp'), parts along dimension 1
The draws below stay inside these ranges and needn't reach their ends.
There are 2 independent parts, one for each index of `groups`. The reference program is written for one: setup_inputs(seed, part) draws one part's arguments, and reference() takes and returns one part's arrays. A program takes and returns all parts, laid end to end along the dimension named above; an argument that names none is the same for every part. Nothing has to cross between parts.
Inputs may be any that keep to these rules, and one draw needn't show every extreme that they name: For every instance and m, the slots page_table[r, j, m] of the instance's 8 requests and mig_slots[i, u, j, m] together name every slot of block m exactly once. `mig_slots`: see page_table. mig_dest[i, u] differs from i; every instance receives exactly 2 requests; in every draw some instance sends exactly 1 request to one other and none sends more. The pairs (mig_dest, mig_local) name distinct requests.
All inputs are finite; a program needn't handle non-finite values. No bound on the sum of `lengths` on one device may be relied on, other than what follows from the above.
Results may differ from the reference program's by a relative error of at most 0.0035.
Values may be sent and summed in bfloat16 or wider, within the bound.
A program may use at most 64 MiB of HBM per device.

```python
import math
import jax
import jax.numpy as jnp
import numpy as np
from jax import lax

D = 5120
QH = 32
KVH = 4
HD = 128
PAGE = 16
STEPS = 3
R_INST = 8
PPD = 1
REQS = 32
MIG_SRC = 2
CTX = 64
POOL_DEV = 10
N_INST = 4
N_MP = 4


def slot_order(key):
    key = jax.random.fold_in(key, 7)
    scores = jax.random.randint(key, (N_INST, N_MP, POOL_DEV), 0, 1 << 20)
    scores = scores * POOL_DEV + jnp.arange(POOL_DEV, dtype=jnp.int32)
    return jnp.argsort(scores, axis=-1).astype(jnp.int32)


def migration_plan(key):
    key = jax.random.fold_in(key, 11)
    first, second, third = jax.random.split(key, 3)
    offsets = 1 + jax.random.permutation(first, N_INST - 1).astype(jnp.int32)
    shifted = offsets[jnp.arange(MIG_SRC, dtype=jnp.int32) % (N_INST - 1)]
    shuffle = jax.random.permutation(third, N_INST).astype(jnp.int32)
    placing = jnp.argsort(shuffle).astype(jnp.int32)
    target_inst = shuffle[(placing[:, None] + shifted[None, :]) % N_INST]
    scores = jax.random.randint(second, (N_INST, R_INST), 0, 1 << 20) * R_INST + jnp.arange(R_INST, dtype=jnp.int32)
    orders = jnp.argsort(scores, axis=-1).astype(jnp.int32)
    local_index = orders[target_inst, jnp.arange(MIG_SRC, dtype=jnp.int32)[None, :]]
    return (target_inst, local_index)


def common_direction(key):
    return jax.random.uniform(jax.random.fold_in(key, 5), (HD,), minval=-1.0, maxval=1.0)


def draw_page_table(key, part):
    order = slot_order(key)
    used = order[:, :, :R_INST * PPD].reshape(N_INST, N_MP, R_INST, PPD)
    return jnp.transpose(used, (0, 2, 3, 1)).reshape(REQS, PPD, N_MP)


def draw_mig_slots(key, part):
    order = slot_order(key)
    spare = order[:, :, R_INST * PPD:].reshape(N_INST, N_MP, MIG_SRC, PPD)
    return jnp.transpose(spare, (0, 2, 3, 1))


def draw_mig_dest(key, part):
    target_inst, local_index = migration_plan(key)
    return target_inst


def draw_mig_local(key, part):
    target_inst, local_index = migration_plan(key)
    return local_index


def draw_kv_pool(key, part):
    direction = common_direction(key)
    key = jax.random.fold_in(key, 1)
    shape = (N_INST, N_MP * POOL_DEV, PAGE, KVH, 2, HD)
    noise = jnp.clip(jax.random.normal(key, shape), -6.0, 6.0)
    keys = jnp.clip(2.0 * direction + 0.5 * noise[..., 0, :], -6.0, 6.0)
    whole = jnp.stack([keys, noise[..., 1, :]], axis=-2)
    return whole.reshape(N_INST, N_MP * POOL_DEV, PAGE, KVH * 2 * HD).astype(jnp.bfloat16)


def draw_queries(key, part):
    direction = common_direction(key)
    key = jax.random.fold_in(key, 2)
    first, second, third = jax.random.split(key, 3)
    shape = (STEPS, REQS, QH, HD)
    strong = jax.random.uniform(second, (STEPS, REQS, 1, 1)) < 0.2
    strength = jax.random.uniform(third, (STEPS, REQS, 1, 1), minval=5.0, maxval=120.0)
    base = jnp.clip(jax.random.normal(first, shape), -6.0, 6.0)
    whole = base + jnp.where(strong, strength, 0.0) * direction
    return whole.reshape(STEPS, REQS, QH * HD).astype(jnp.bfloat16)


def shard_levels(key, dims, cuts, least, high):
    def one(axis_at, shards_of):
        draws = jax.random.uniform(jax.random.fold_in(jax.random.fold_in(key, 6), axis_at), (shards_of,), jnp.float32, least / len(cuts), high / len(cuts))
        return jnp.repeat(jnp.exp(draws), dims[axis_at] // shards_of).reshape((-1,) + (1,) * (len(dims) - axis_at - 1))

    loudness = one(*cuts[0])
    for cut in cuts[1:]:
        loudness = loudness * one(*cut)
    return loudness


def profile(count, total, most, lean):
    portions = [(1 << 20) // math.isqrt(grade ** lean) + 1 for grade in range(2, count + 1)]
    spare, given = total - most - (count - 1), [1] * (count - 1)
    while spare > 0:
        candidates = [i for i in range(count - 1) if given[i] < most]
        whole, budget = sum([portions[i] for i in candidates]), spare
        for i in candidates:
            extra = min(most - given[i], max(1, budget * portions[i] // whole), spare)
            given[i] = given[i] + extra
            spare = spare - extra
    return np.array([most] + given)


def uneven(own_key, count, total, limit, slope):
    if count == 2:
        one = jax.random.randint(own_key, (), max(1, total - limit), min(limit, total - 1) + 1)
        return jnp.stack([one, total - one])
    sizes = jnp.asarray(profile(count, total, limit, slope), jnp.int32)
    couples = (count - 1) // 2
    giver, sink = sizes[1:1 + 2 * couples:2], sizes[2:2 + 2 * couples:2]
    room = jnp.minimum(giver - 1, limit - sink)
    moved = jax.random.randint(jax.random.fold_in(own_key, 1), (couples,), 0, 1 << 20) % (room + 1)
    sizes = sizes.at[1:1 + 2 * couples:2].set(giver - moved).at[2:2 + 2 * couples:2].set(sink + moved)
    return sizes[jax.random.permutation(jax.random.fold_in(own_key, 2), count)]


def normal_values(rng, shape, spread, most, shards=(), kind=jnp.bfloat16):
    factor_of = shard_levels(rng, shape, shards, -0.22, 0.18) if shards else 1.0
    drawn = jax.random.normal(rng, shape, jnp.float32) * spread * factor_of
    return jnp.minimum(jnp.maximum(drawn, -most), most).astype(kind)


def setup_inputs(seed: int = 0, part: int = 0) -> dict:
    seeds = jax.random.split(jax.random.key(seed), 11)
    part_splits = jax.random.split(jax.random.fold_in(seeds[10], part), 11)
    hidden_states = normal_values(part_splits[0], (STEPS, REQS, D), 1.0, 6.0, ((1, 4), (2, 4)))
    kv_weight = normal_values(seeds[1], (D, KVH * 2 * HD), D ** -0.5, 0.078125, ((0, 4),))
    key_gain = jnp.clip(1.0 + 0.18 * jax.random.normal(seeds[2], (HD,), jnp.float32), 0.1, 1.9)
    queries = draw_queries(jax.random.fold_in(jax.random.fold_in(seeds[10], part), 71), part)
    kv_pool = draw_kv_pool(jax.random.fold_in(jax.random.fold_in(seeds[10], part), 71), part)
    page_table = draw_page_table(jax.random.fold_in(jax.random.fold_in(seeds[10], part), 71), part)
    lengths = uneven(part_splits[6], REQS, REQS * (CTX - STEPS) // 2, CTX - STEPS, 2).astype(jnp.int32)
    mig_dest = draw_mig_dest(jax.random.fold_in(jax.random.fold_in(seeds[10], part), 71), part)
    mig_local = draw_mig_local(jax.random.fold_in(jax.random.fold_in(seeds[10], part), 71), part)
    mig_slots = draw_mig_slots(jax.random.fold_in(jax.random.fold_in(seeds[10], part), 71), part)
    return dict(hidden_states=hidden_states, kv_weight=kv_weight, key_gain=key_gain, queries=queries, kv_pool=kv_pool, page_table=page_table, lengths=lengths, mig_dest=mig_dest, mig_local=mig_local, mig_slots=mig_slots)


def rotary(keys, positions):
    half = keys.shape[-1] // 2
    freq = jnp.exp(-(2.0 * jnp.arange(half).astype(jnp.float32) / keys.shape[-1]) * math.log(1000000.0))
    angle = positions.astype(jnp.float32)[..., None] * freq
    cosine = jnp.cos(angle)
    sine = jnp.sin(angle)
    first = keys[..., :half]
    second = keys[..., half:]
    return jnp.concatenate([first * cosine - second * sine, second * cosine + first * sine], axis=-1)

def new_entries(projected, key_gain, positions):
    keys = projected[..., 0, :]
    values = projected[..., 1, :]
    factor = lax.rsqrt(lax.optimization_barrier(jnp.mean(keys * keys, axis=-1, keepdims=True)) + 1e-06)
    keys = rotary(keys * factor * key_gain, positions[:, :, None])
    return jnp.stack([keys, values], axis=-2).reshape(positions.shape + (-1,)).astype(jnp.bfloat16)

def reference(hidden_states, kv_weight, key_gain, queries, kv_pool, page_table, lengths, mig_dest, mig_local, mig_slots):
    width = KVH * 2 * HD
    pool = kv_pool.reshape(N_INST, N_MP, POOL_DEV, PAGE, width)
    source = jnp.arange(N_INST).astype(jnp.int32)[:, None, None, None]
    column = jnp.arange(N_MP).astype(jnp.int32)[None, None, None, :]
    moving = pool[source, column, mig_slots]
    request = mig_dest * R_INST + mig_local
    targets = page_table[request]
    pool = pool.at[mig_dest[:, :, None, None], column, targets].set(moving)
    projected = jnp.dot(hidden_states.reshape(STEPS * REQS, D), kv_weight, preferred_element_type=jnp.float32)
    projected = projected.reshape(STEPS, REQS, KVH, 2, HD)
    positions = lengths[None, :] + jnp.arange(STEPS).astype(jnp.int32)[:, None]
    fresh = new_entries(projected, key_gain, positions)
    page_number = positions // PAGE
    holder = page_number % N_MP
    deeper = page_number // N_MP
    offset = positions % PAGE
    requests = jnp.arange(REQS).astype(jnp.int32)
    slot_index = page_table[requests[None, :], deeper, holder]
    owner = jnp.broadcast_to((requests // R_INST)[None, :], positions.shape)
    pool = pool.at[owner, holder, slot_index, offset].set(fresh)

    def one_instance(index):
        pool_here = lax.dynamic_index_in_dim(pool, index, 0, keepdims=False)
        table = lax.dynamic_slice_in_dim(page_table, index * R_INST, R_INST, 0)
        reach = lax.dynamic_slice_in_dim(positions, index * R_INST, R_INST, 1)
        query = lax.dynamic_slice_in_dim(queries, index * R_INST, R_INST, 1).astype(jnp.float32)
        query = query.reshape(STEPS, R_INST, KVH, QH // KVH, HD)
        blocks = jnp.arange(N_MP).astype(jnp.int32)[None, None, :]
        cached = pool_here[blocks, table].reshape(R_INST, CTX, KVH, 2, HD).astype(jnp.float32)
        scores = jnp.einsum('trhgd,rkhd->trhgk', query, cached[..., 0, :], precision=lax.Precision.HIGHEST) / math.sqrt(HD)
        valid = (jnp.arange(CTX).astype(jnp.int32)[None, None, :] <= reach[:, :, None])[:, :, None, None, :]
        scores = jnp.where(valid, scores, -1e+30)
        peak = lax.optimization_barrier(jnp.max(scores, axis=-1))
        weights = jnp.where(valid, jnp.exp(scores - peak[..., None]), 0.0)
        total = lax.optimization_barrier(jnp.sum(weights, axis=-1))
        summed = jnp.einsum('trhgk,rkhd->trhgd', weights, cached[..., 1, :], precision=lax.Precision.HIGHEST)
        result = (summed / total[..., None]).reshape(STEPS, R_INST, QH * HD)
        return result.astype(jnp.bfloat16)
    outputs = lax.map(one_instance, jnp.arange(N_INST).astype(jnp.int32))
    return jnp.transpose(outputs, (1, 0, 2, 3)).reshape(STEPS, REQS, QH * HD)
```

```python
import functools
import math

import jax
import jax.numpy as jnp
from jax import lax
from jax.experimental import pallas as pl
from jax.experimental.pallas import tpu as pltpu
from jax.sharding import PartitionSpec as P

MESH = pl.DeviceIdType.MESH
F32 = jnp.float32
BF16 = jnp.bfloat16


def loop(count, step):
    if count <= 4:
        for index in range(count):
            step(index)
    else:
        lax.fori_loop(0, count, lambda index, carry: (step(index), carry)[1], 0)


def dot(left, right, contract=((1,), (0,))):
    return lax.dot_general(left, right, (contract, ((), ())), preferred_element_type=F32)


def weighted(weights, values):
    high = weights.astype(BF16)
    low = (weights - high.astype(F32)).astype(BF16)
    return dot(high, values) + dot(low, values)


def kernel(
    n_inst,
    n_mp,
    migrants,
    kv_heads,
    ints,
    hidden,
    weight,
    gain,
    queries,
    pool,
    out,
    pool_v,
    hidden_v,
    weight_v,
    gain_v,
    query_v,
    stage,
    leaving,
    cache,
    part_out,
    part_in,
    key_all,
    value_all,
    in_sem,
    weight_sem,
    own_sem,
    page_send,
    page_recv,
    mig_send,
    mig_recv,
    part_send,
    part_recv,
):
    inst = lax.axis_index("inst")
    mp = lax.axis_index("mp")
    steps, requests, _ = hidden.shape
    head_dim = gain.shape[1]
    pair = 2 * head_dim
    page = pool.shape[1]
    rows = steps * requests
    portion = query_v.shape[2] // head_dim
    share = n_mp // kv_heads
    context = n_mp * page
    own_head = mp // share

    def columns(head):
        return pl.ds(pl.multiple_of(head * pair, pair), pair)

    loads = [
        pltpu.make_async_copy(pool, pool_v, in_sem.at[0]),
        pltpu.make_async_copy(hidden, hidden_v, in_sem.at[1]),
        pltpu.make_async_copy(
            queries.at[
                :,
                :,
                pl.ds(pl.multiple_of(mp * (portion * head_dim), head_dim), portion * head_dim),
            ],
            query_v,
            in_sem.at[2],
        ),
        pltpu.make_async_copy(gain, gain_v, in_sem.at[3]),
    ]
    heads = [lax.rem(own_head + 1 + j, kv_heads) for j in range(kv_heads)]
    weight_loads = [
        pltpu.make_async_copy(weight.at[:, columns(head)], weight_v.at[j], weight_sem.at[j])
        for j, head in enumerate(heads)
    ]
    loads[0].start()
    loads[1].start()
    for load in weight_loads:
        load.start()
    loads[2].start()
    loads[3].start()

    barrier = pltpu.get_barrier_semaphore()

    def greet_instance(away, to_inst):
        def greet(other):
            pl.semaphore_signal(
                barrier, inc=1, device_id={"inst": to_inst, "mp": other}, device_id_type=MESH
            )

        loop(n_mp, greet)

    def greet_peer(k):
        pl.semaphore_signal(
            barrier,
            inc=1,
            device_id={"inst": inst, "mp": lax.rem(mp + 1 + k, n_mp)},
            device_id_type=MESH,
        )

    loop(n_mp - 1, greet_peer)
    loop(n_inst - 1, lambda k: greet_instance(k, lax.rem(inst + 1 + k, n_inst)))

    table_at, length_at, dest_at = 0, requests, 2 * requests
    local_at = dest_at + n_inst * migrants
    slot_at = local_at + n_inst * migrants

    loads[0].wait()
    for r in range(requests):
        stage[r] = pool_v[ints[table_at + r]]

    def take_leaving(k):
        to_inst = lax.rem(inst + 1 + k, n_inst)
        slot = ints[slot_at]
        for u in range(1, migrants):
            slot = jnp.where(
                ints[dest_at + inst * migrants + u] == to_inst, ints[slot_at + u], slot
            )
        leaving[k] = pool_v[slot]

    loop(n_inst - 1, take_leaving)

    def page_copy(k):
        to = lax.rem(mp + 1 + k, n_mp)
        return pltpu.make_async_remote_copy(
            src_ref=stage.at[:, :, columns(to // share)],
            dst_ref=cache.at[pl.ds(0, requests), mp],
            send_sem=page_send.at[k],
            recv_sem=page_recv.at[k],
            device_id={"inst": inst, "mp": to},
            device_id_type=MESH,
        )

    def mig_copy(k, to, column):
        return pltpu.make_async_remote_copy(
            src_ref=leaving.at[k, :, columns(to // share)],
            dst_ref=cache.at[requests + k, column],
            send_sem=mig_send.at[k, to],
            recv_sem=mig_recv.at[k, column],
            device_id={"inst": lax.rem(inst + 1 + k, n_inst), "mp": to},
            device_id_type=MESH,
        )

    def part_copy(j, k):
        to = lax.rem(mp + 1 + k, n_mp)
        return pltpu.make_async_remote_copy(
            src_ref=part_out.at[j],
            dst_ref=part_in.at[k],
            send_sem=part_send.at[k],
            recv_sem=part_recv.at[k],
            device_id={"inst": inst, "mp": to},
            device_id_type=MESH,
        )

    own_copy = pltpu.make_async_copy(
        stage.at[:, :, columns(own_head)], cache.at[pl.ds(0, requests), mp], own_sem
    )
    own_copy.start()

    pl.semaphore_wait(barrier, n_inst * n_mp - 1)
    loop(n_mp - 1, lambda k: page_copy(k).start())
    loop(n_inst - 1, lambda k: loop(n_mp, lambda to: mig_copy(k, to, mp).start()))

    loads[1].wait()
    features = hidden_v[...].astype(F32).reshape(rows, hidden.shape[2]).astype(BF16)
    for j in range(kv_heads):
        weight_loads[j].wait()
        part_out[j] = dot(features, weight_v[j])
        if share == 1:
            if j < kv_heads - 1:
                part_copy(j, j).start()
    if share > 1:

        def send_part(k):
            to = lax.rem(mp + 1 + k, n_mp)
            j = lax.rem(to // share - own_head - 1 + 2 * kv_heads, kv_heads)
            part_copy(j, k).start()

        loop(n_mp - 1, send_part)

    block = [jnp.int32(r) for r in range(requests)]
    for k in range(n_inst - 1):
        source = lax.rem(inst + 2 * n_inst - 1 - k, n_inst)
        place = jnp.int32(-1)
        for u in range(migrants):
            at = source * migrants + u
            place = jnp.where(ints[dest_at + at] == inst, ints[local_at + at], place)
        for r in range(requests):
            block[r] = jnp.where(place == r, requests + k, block[r])

    row8 = lax.broadcasted_iota(jnp.int32, (requests, head_dim), 0)
    length8 = jnp.zeros((requests, head_dim), jnp.int32)
    for r in range(requests):
        length8 = jnp.where(row8 == r, ints[length_at + r], length8)

    half = head_dim // 2
    lane = lax.broadcasted_iota(jnp.int32, (rows, head_dim), 1)
    pair_index = jnp.where(lane < half, lane, lane - half)
    frequency = jnp.exp(-(2.0 * pair_index.astype(F32) / head_dim) * math.log(1000000.0))
    place = jnp.concatenate([(length8 + t).astype(F32) for t in range(steps)], axis=0)
    angle = place * frequency
    cosine = jnp.cos(angle)
    sine = jnp.sin(angle)
    sine = jnp.where(lane < half, -sine, sine)

    cached_lane = lax.broadcasted_iota(jnp.int32, (requests, requests * context), 1)
    first = lax.broadcasted_iota(jnp.int32, (requests, requests * context), 0) * context
    last = first + jnp.broadcast_to(length8[:, :1], first.shape)
    bias = jnp.where((cached_lane >= first) & (cached_lane < last), 0.0, -1e30).astype(F32)

    row = lax.broadcasted_iota(jnp.int32, (rows, 128), 0)
    column = lax.broadcasted_iota(jnp.int32, (rows, 128), 1)
    fresh_bias = jnp.where(
        (lax.rem(row, requests) == lax.rem(column, requests)) & (column <= row), 0.0, -1e30
    ).astype(F32)

    loads[2].wait()
    query = jnp.concatenate(
        [
            query_v[t, :, g * head_dim : (g + 1) * head_dim].astype(F32)
            for g in range(portion)
            for t in range(steps)
        ],
        axis=0,
    ).astype(BF16)
    value_all[:, head_dim:] = jnp.ones((requests * context, head_dim), BF16)
    scale = 1.0 / math.sqrt(head_dim)

    own_copy.wait()
    loop(n_mp - 1, lambda k: page_copy(k).wait_recv())
    loop(n_inst - 1, lambda k: loop(n_mp, lambda to: mig_copy(k, to, to).wait_recv()))
    for r in range(requests):
        held = cache[block[r]].reshape(context, pair)
        key_all[r * context : (r + 1) * context, :] = held[:, :head_dim]
        value_all[r * context : (r + 1) * context, :head_dim] = held[:, head_dim:]

    total_rows = portion * rows
    scores = dot(query, key_all[...], ((1,), (1,))) * scale
    scores = scores.reshape(portion * steps, requests, requests * context) + bias[None]
    scores = scores.reshape(total_rows, requests * context)
    peak = jnp.max(scores, axis=-1, keepdims=True)
    summed = weighted(jnp.exp(scores - peak), value_all[...])

    loads[3].wait()
    loop(n_mp - 1, lambda k: part_copy(0, k).wait_recv())
    projected = part_out[kv_heads - 1]
    for k in range(n_mp - 1):
        projected = projected + part_in[k]
    keys = projected[:, :head_dim]
    factor = lax.rsqrt(jnp.mean(keys * keys, axis=-1, keepdims=True) + 1e-06)
    keys = keys * factor * gain_v[...]
    keys = keys * cosine + pltpu.roll(keys, half, 1) * sine
    blank = jnp.zeros((128 - rows, head_dim), F32)
    fresh_keys = jnp.concatenate([keys, blank], axis=0).astype(BF16)
    fresh_values = jnp.concatenate([projected[:, head_dim:], blank], axis=0).astype(BF16)
    fresh_values = jnp.concatenate(
        [fresh_values, jnp.ones((128, head_dim), BF16)], axis=1
    )
    fresh = dot(query, fresh_keys, ((1,), (1,))) * scale
    fresh = (fresh.reshape(portion, rows, 128) + fresh_bias[None]).reshape(total_rows, 128)
    highest = jnp.maximum(peak, jnp.max(fresh, axis=-1, keepdims=True))
    summed = summed * jnp.exp(peak - highest) + weighted(jnp.exp(fresh - highest), fresh_values)
    result = summed[:, :head_dim] / summed[:, head_dim:]
    for t in range(steps):
        for g in range(portion):
            at = (g * steps + t) * requests
            out[t, :, g * head_dim : (g + 1) * head_dim] = result[at : at + requests].astype(BF16)

    loop(n_mp - 1, lambda k: page_copy(k).wait_send())
    loop(n_inst - 1, lambda k: loop(n_mp, lambda to: mig_copy(k, to, mp).wait_send()))
    loop(n_mp - 1, lambda k: part_copy(0, k).wait_send())


def local(
    n_inst,
    n_mp,
    hidden_states,
    kv_weight,
    key_gain,
    queries,
    kv_pool,
    page_table,
    lengths,
    mig_dest,
    mig_local,
    mig_slots,
):
    steps, requests, depth = hidden_states.shape
    head_dim = key_gain.shape[0]
    width = kv_weight.shape[1]
    pair = 2 * head_dim
    kv_heads = width // pair
    portion = queries.shape[2] // n_mp
    migrants = mig_dest.shape[1]
    pool = kv_pool[0]
    page = pool.shape[1]
    rows = steps * requests
    context = n_mp * page
    assert page_table.shape[1] == 1 and n_mp % kv_heads == 0
    ints = jnp.concatenate(
        [
            page_table.reshape(-1),
            lengths,
            mig_dest.reshape(-1),
            mig_local.reshape(-1),
            mig_slots.reshape(-1),
        ]
    )
    anywhere = pl.BlockSpec(memory_space=pl.ANY)
    return pl.pallas_call(
        functools.partial(kernel, n_inst, n_mp, migrants, kv_heads),
        out_shape=jax.ShapeDtypeStruct((steps, requests, portion), BF16),
        in_specs=[pl.BlockSpec(memory_space=pltpu.SMEM)] + [anywhere] * 5,
        out_specs=pl.BlockSpec(memory_space=pltpu.VMEM),
        scratch_shapes=[
            pltpu.VMEM(pool.shape, BF16),
            pltpu.VMEM(hidden_states.shape, BF16),
            pltpu.VMEM((kv_heads, depth, pair), BF16),
            pltpu.VMEM((1, head_dim), F32),
            pltpu.VMEM((steps, requests, portion), BF16),
            pltpu.VMEM((requests, page, width), BF16),
            pltpu.VMEM((n_inst - 1, page, width), BF16),
            pltpu.VMEM((requests + n_inst - 1, n_mp, page, pair), BF16),
            pltpu.VMEM((kv_heads, rows, pair), F32),
            pltpu.VMEM((n_mp - 1, rows, pair), F32),
            pltpu.VMEM((requests * context, head_dim), BF16),
            pltpu.VMEM((requests * context, pair), BF16),
            pltpu.SemaphoreType.DMA((4,)),
            pltpu.SemaphoreType.DMA((kv_heads,)),
            pltpu.SemaphoreType.DMA,
            pltpu.SemaphoreType.DMA((n_mp - 1,)),
            pltpu.SemaphoreType.DMA((n_mp - 1,)),
            pltpu.SemaphoreType.DMA((n_inst - 1, n_mp)),
            pltpu.SemaphoreType.DMA((n_inst - 1, n_mp)),
            pltpu.SemaphoreType.DMA((n_mp - 1,)),
            pltpu.SemaphoreType.DMA((n_mp - 1,)),
        ],
        compiler_params=pltpu.CompilerParams(
            collective_id=0, has_side_effects=True, vmem_limit_bytes=32 * 1024 * 1024
        ),
    )(ints, hidden_states, kv_weight, key_gain.reshape(1, head_dim), queries, pool)


def solution(mesh):
    placed = (
        P(None, ("groups", "inst"), "mp"),
        P("mp", None),
        P(),
        P(None, ("groups", "inst"), None),
        P(("groups", "inst"), "mp", None, None),
        P(("groups", "inst"), None, "mp"),
        P(("groups", "inst")),
        P("groups", None),
        P("groups", None),
        P(("groups", "inst"), None, None, "mp"),
    )
    return jax.shard_map(
        functools.partial(local, mesh.shape["inst"], mesh.shape["mp"]),
        mesh=mesh,
        in_specs=placed,
        out_specs=P(None, ("groups", "inst"), "mp"),
        check_vma=False,
    )
```

```python
import functools
import math

import jax
import jax.numpy as jnp
from jax import lax
from jax.experimental import pallas as pl
from jax.experimental.pallas import tpu as pltpu
from jax.sharding import PartitionSpec as P

MESH = pl.DeviceIdType.MESH
F32 = jnp.float32
BF16 = jnp.bfloat16


def loop(count, step):
    if count <= 4:
        for index in range(count):
            step(index)
    else:
        lax.fori_loop(0, count, lambda index, carry: (step(index), carry)[1], 0)


def dot(left, right, contract=((1,), (0,))):
    return lax.dot_general(left, right, (contract, ((), ())), preferred_element_type=F32)


def weighted(weights, values):
    high = weights.astype(BF16)
    low = (weights - high.astype(F32)).astype(BF16)
    return dot(high, values) + dot(low, values)


def kernel(
    n_inst,
    n_mp,
    migrants,
    kv_heads,
    table_h,
    length_h,
    dest_h,
    local_h,
    slot_h,
    hidden,
    weight,
    gain,
    queries,
    pool,
    out,
    pool_v,
    hidden_v,
    weight_v,
    gain_v,
    query_v,
    stage,
    leaving,
    cache,
    part_out,
    part_in,
    key_all,
    value_all,
    table,
    length,
    mig_dest,
    mig_local,
    mig_slot,
    int_sem,
    in_sem,
    weight_sem,
    own_sem,
    page_send,
    page_recv,
    mig_send,
    mig_recv,
    part_send,
    part_recv,
):
    inst = lax.axis_index("inst")
    mp = lax.axis_index("mp")
    steps, requests, _ = hidden.shape
    head_dim = gain.shape[1]
    pair = 2 * head_dim
    page = pool.shape[1]
    rows = steps * requests
    portion = query_v.shape[2] // head_dim
    share = n_mp // kv_heads
    context = n_mp * page
    own_head = mp // share

    def columns(head):
        return pl.ds(pl.multiple_of(head * pair, pair), pair)

    loads = [
        pltpu.make_async_copy(pool, pool_v, in_sem.at[0]),
        pltpu.make_async_copy(hidden, hidden_v, in_sem.at[1]),
        pltpu.make_async_copy(
            queries.at[
                :,
                :,
                pl.ds(pl.multiple_of(mp * (portion * head_dim), head_dim), portion * head_dim),
            ],
            query_v,
            in_sem.at[2],
        ),
        pltpu.make_async_copy(gain, gain_v, in_sem.at[3]),
    ]
    heads = [lax.rem(own_head + 1 + j, kv_heads) for j in range(kv_heads)]
    weight_loads = [
        pltpu.make_async_copy(weight.at[:, columns(head)], weight_v.at[j], weight_sem.at[j])
        for j, head in enumerate(heads)
    ]
    int_loads = [
        pltpu.make_async_copy(source, target, int_sem.at[n])
        for n, (source, target) in enumerate(
            [
                (table_h, table),
                (slot_h, mig_slot),
                (dest_h, mig_dest),
                (local_h, mig_local),
                (length_h, length),
            ]
        )
    ]
    loads[0].start()
    for load in int_loads:
        load.start()
    loads[1].start()
    for load in weight_loads:
        load.start()
    loads[2].start()
    loads[3].start()

    barrier = pltpu.get_barrier_semaphore()

    def greet_instance(away, to_inst):
        def greet(other):
            pl.semaphore_signal(
                barrier, inc=1, device_id={"inst": to_inst, "mp": other}, device_id_type=MESH
            )

        loop(n_mp, greet)

    def greet_peer(k):
        pl.semaphore_signal(
            barrier,
            inc=1,
            device_id={"inst": inst, "mp": lax.rem(mp + 1 + k, n_mp)},
            device_id_type=MESH,
        )

    loop(n_mp - 1, greet_peer)
    loop(n_inst - 1, lambda k: greet_instance(k, lax.rem(inst + 1 + k, n_inst)))

    for load in int_loads:
        load.wait()
    loads[0].wait()
    for r in range(requests):
        stage[r] = pool_v[table[r]]

    def take_leaving(k):
        to_inst = lax.rem(inst + 1 + k, n_inst)
        slot = mig_slot[0]
        for u in range(1, migrants):
            slot = jnp.where(mig_dest[u, inst] == to_inst, mig_slot[u], slot)
        leaving[k] = pool_v[slot]

    loop(n_inst - 1, take_leaving)

    def page_copy(k):
        to = lax.rem(mp + 1 + k, n_mp)
        return pltpu.make_async_remote_copy(
            src_ref=stage.at[:, :, columns(to // share)],
            dst_ref=cache.at[pl.ds(0, requests), mp],
            send_sem=page_send.at[k],
            recv_sem=page_recv.at[k],
            device_id={"inst": inst, "mp": to},
            device_id_type=MESH,
        )

    def mig_copy(k, to, column):
        return pltpu.make_async_remote_copy(
            src_ref=leaving.at[k, :, columns(to // share)],
            dst_ref=cache.at[requests + k, column],
            send_sem=mig_send.at[k, to],
            recv_sem=mig_recv.at[k, column],
            device_id={"inst": lax.rem(inst + 1 + k, n_inst), "mp": to},
            device_id_type=MESH,
        )

    def part_copy(j, k):
        to = lax.rem(mp + 1 + k, n_mp)
        return pltpu.make_async_remote_copy(
            src_ref=part_out.at[j],
            dst_ref=part_in.at[k],
            send_sem=part_send.at[k],
            recv_sem=part_recv.at[k],
            device_id={"inst": inst, "mp": to},
            device_id_type=MESH,
        )

    own_copy = pltpu.make_async_copy(
        stage.at[:, :, columns(own_head)], cache.at[pl.ds(0, requests), mp], own_sem
    )
    own_copy.start()

    pl.semaphore_wait(barrier, n_inst * n_mp - 1)
    loop(n_mp - 1, lambda k: page_copy(k).start())
    loop(n_inst - 1, lambda k: loop(n_mp, lambda to: mig_copy(k, to, mp).start()))

    loads[1].wait()
    features = hidden_v[...].astype(F32).reshape(rows, hidden.shape[2]).astype(BF16)
    for j in range(kv_heads):
        weight_loads[j].wait()
        part_out[j] = dot(features, weight_v[j])
        if share == 1:
            if j < kv_heads - 1:
                part_copy(j, j).start()
    if share > 1:

        def send_part(k):
            to = lax.rem(mp + 1 + k, n_mp)
            j = lax.rem(to // share - own_head - 1 + 2 * kv_heads, kv_heads)
            part_copy(j, k).start()

        loop(n_mp - 1, send_part)

    block = [jnp.int32(r) for r in range(requests)]
    for k in range(n_inst - 1):
        source = lax.rem(inst + 2 * n_inst - 1 - k, n_inst)
        place = jnp.int32(-1)
        for u in range(migrants):
            place = jnp.where(mig_dest[u, source] == inst, mig_local[u, source], place)
        for r in range(requests):
            block[r] = jnp.where(place == r, requests + k, block[r])

    row8 = lax.broadcasted_iota(jnp.int32, (requests, head_dim), 0)
    length8 = jnp.zeros((requests, head_dim), jnp.int32)
    for r in range(requests):
        length8 = jnp.where(row8 == r, length[r], length8)

    half = head_dim // 2
    lane = lax.broadcasted_iota(jnp.int32, (rows, head_dim), 1)
    pair_index = jnp.where(lane < half, lane, lane - half)
    frequency = jnp.exp(-(2.0 * pair_index.astype(F32) / head_dim) * math.log(1000000.0))
    place = jnp.concatenate([(length8 + t).astype(F32) for t in range(steps)], axis=0)
    angle = place * frequency
    cosine = jnp.cos(angle)
    sine = jnp.sin(angle)
    sine = jnp.where(lane < half, -sine, sine)

    cached_lane = lax.broadcasted_iota(jnp.int32, (requests, requests * context), 1)
    first = lax.broadcasted_iota(jnp.int32, (requests, requests * context), 0) * context
    last = first + jnp.broadcast_to(length8[:, :1], first.shape)
    bias = jnp.where((cached_lane >= first) & (cached_lane < last), 0.0, -1e30).astype(F32)

    row = lax.broadcasted_iota(jnp.int32, (rows, 128), 0)
    column = lax.broadcasted_iota(jnp.int32, (rows, 128), 1)
    fresh_bias = jnp.where(
        (lax.rem(row, requests) == lax.rem(column, requests)) & (column <= row), 0.0, -1e30
    ).astype(F32)

    loads[2].wait()
    query = jnp.concatenate(
        [
            query_v[t, :, g * head_dim : (g + 1) * head_dim].astype(F32)
            for g in range(portion)
            for t in range(steps)
        ],
        axis=0,
    ).astype(BF16)
    value_all[:, head_dim:] = jnp.ones((requests * context, head_dim), BF16)
    scale = 1.0 / math.sqrt(head_dim)

    own_copy.wait()
    loop(n_mp - 1, lambda k: page_copy(k).wait_recv())
    loop(n_inst - 1, lambda k: loop(n_mp, lambda to: mig_copy(k, to, to).wait_recv()))
    for r in range(requests):
        held = cache[block[r]].reshape(context, pair)
        key_all[r * context : (r + 1) * context, :] = held[:, :head_dim]
        value_all[r * context : (r + 1) * context, :head_dim] = held[:, head_dim:]

    total_rows = portion * rows
    scores = dot(query, key_all[...], ((1,), (1,))) * scale
    scores = scores.reshape(portion * steps, requests, requests * context) + bias[None]
    scores = scores.reshape(total_rows, requests * context)
    peak = jnp.max(scores, axis=-1, keepdims=True)
    summed = weighted(jnp.exp(scores - peak), value_all[...])

    loads[3].wait()
    loop(n_mp - 1, lambda k: part_copy(0, k).wait_recv())
    projected = part_out[kv_heads - 1]
    for k in range(n_mp - 1):
        projected = projected + part_in[k]
    keys = projected[:, :head_dim]
    factor = lax.rsqrt(jnp.mean(keys * keys, axis=-1, keepdims=True) + 1e-06)
    keys = keys * factor * gain_v[...]
    keys = keys * cosine + pltpu.roll(keys, half, 1) * sine
    blank = jnp.zeros((128 - rows, head_dim), F32)
    fresh_keys = jnp.concatenate([keys, blank], axis=0).astype(BF16)
    fresh_values = jnp.concatenate([projected[:, head_dim:], blank], axis=0).astype(BF16)
    fresh_values = jnp.concatenate(
        [fresh_values, jnp.ones((128, head_dim), BF16)], axis=1
    )
    fresh = dot(query, fresh_keys, ((1,), (1,))) * scale
    fresh = (fresh.reshape(portion, rows, 128) + fresh_bias[None]).reshape(total_rows, 128)
    highest = jnp.maximum(peak, jnp.max(fresh, axis=-1, keepdims=True))
    summed = summed * jnp.exp(peak - highest) + weighted(jnp.exp(fresh - highest), fresh_values)
    result = summed[:, :head_dim] / summed[:, head_dim:]
    for t in range(steps):
        for g in range(portion):
            at = (g * steps + t) * requests
            out[t, :, g * head_dim : (g + 1) * head_dim] = result[at : at + requests].astype(BF16)

    loop(n_mp - 1, lambda k: page_copy(k).wait_send())
    loop(n_inst - 1, lambda k: loop(n_mp, lambda to: mig_copy(k, to, mp).wait_send()))
    loop(n_mp - 1, lambda k: part_copy(0, k).wait_send())


def local(
    n_inst,
    n_mp,
    hidden_states,
    kv_weight,
    key_gain,
    queries,
    kv_pool,
    page_table,
    lengths,
    mig_dest,
    mig_local,
    mig_slots,
):
    steps, requests, depth = hidden_states.shape
    head_dim = key_gain.shape[0]
    width = kv_weight.shape[1]
    pair = 2 * head_dim
    kv_heads = width // pair
    portion = queries.shape[2] // n_mp
    migrants = mig_dest.shape[1]
    pool = kv_pool[0]
    page = pool.shape[1]
    rows = steps * requests
    context = n_mp * page
    assert page_table.shape[1] == 1 and n_mp % kv_heads == 0
    far = pl.BlockSpec(memory_space=pltpu.HBM)
    return pl.pallas_call(
        functools.partial(kernel, n_inst, n_mp, migrants, kv_heads),
        out_shape=jax.ShapeDtypeStruct((steps, requests, portion), BF16),
        in_specs=[far] * 10,
        out_specs=pl.BlockSpec(memory_space=pltpu.VMEM),
        scratch_shapes=[
            pltpu.VMEM(pool.shape, BF16),
            pltpu.VMEM(hidden_states.shape, BF16),
            pltpu.VMEM((kv_heads, depth, pair), BF16),
            pltpu.VMEM((1, head_dim), F32),
            pltpu.VMEM((steps, requests, portion), BF16),
            pltpu.VMEM((requests, page, width), BF16),
            pltpu.VMEM((n_inst - 1, page, width), BF16),
            pltpu.VMEM((requests + n_inst - 1, n_mp, page, pair), BF16),
            pltpu.VMEM((kv_heads, rows, pair), F32),
            pltpu.VMEM((n_mp - 1, rows, pair), F32),
            pltpu.VMEM((requests * context, head_dim), BF16),
            pltpu.VMEM((requests * context, pair), BF16),
            pltpu.SMEM((requests,), jnp.int32),
            pltpu.SMEM((requests,), jnp.int32),
            pltpu.SMEM((migrants, n_inst), jnp.int32),
            pltpu.SMEM((migrants, n_inst), jnp.int32),
            pltpu.SMEM((migrants,), jnp.int32),
            pltpu.SemaphoreType.DMA((5,)),
            pltpu.SemaphoreType.DMA((4,)),
            pltpu.SemaphoreType.DMA((kv_heads,)),
            pltpu.SemaphoreType.DMA,
            pltpu.SemaphoreType.DMA((n_mp - 1,)),
            pltpu.SemaphoreType.DMA((n_mp - 1,)),
            pltpu.SemaphoreType.DMA((n_inst - 1, n_mp)),
            pltpu.SemaphoreType.DMA((n_inst - 1, n_mp)),
            pltpu.SemaphoreType.DMA((n_mp - 1,)),
            pltpu.SemaphoreType.DMA((n_mp - 1,)),
        ],
        compiler_params=pltpu.CompilerParams(
            collective_id=0, has_side_effects=True, vmem_limit_bytes=32 * 1024 * 1024
        ),
    )(
        page_table.reshape(-1),
        lengths,
        mig_dest.T,
        mig_local.T,
        mig_slots.reshape(-1),
        hidden_states,
        kv_weight,
        key_gain.reshape(1, head_dim),
        queries,
        pool,
    )


def solution(mesh):
    placed = (
        P(None, ("groups", "inst"), "mp"),
        P("mp", None),
        P(),
        P(None, ("groups", "inst"), None),
        P(("groups", "inst"), "mp", None, None),
        P(("groups", "inst"), None, "mp"),
        P(("groups", "inst")),
        P("groups", None),
        P("groups", None),
        P(("groups", "inst"), None, None, "mp"),
    )
    return jax.shard_map(
        functools.partial(local, mesh.shape["inst"], mesh.shape["mp"]),
        mesh=mesh,
        in_specs=placed,
        out_specs=P(None, ("groups", "inst"), "mp"),
        check_vma=False,
    )
```

```python
import functools
import math

import jax
import jax.numpy as jnp
from jax import lax
from jax.experimental import pallas as pl
from jax.experimental.pallas import tpu as pltpu
from jax.sharding import PartitionSpec as P

MESH = pl.DeviceIdType.MESH
F32 = jnp.float32
BF16 = jnp.bfloat16


def loop(count, step):
    if count <= 4:
        for index in range(count):
            step(index)
    else:
        lax.fori_loop(0, count, lambda index, carry: (step(index), carry)[1], 0)


def dot(left, right, contract=((1,), (0,))):
    return lax.dot_general(left, right, (contract, ((), ())), preferred_element_type=F32)


def weighted(weights, values):
    high = weights.astype(BF16)
    low = (weights - high.astype(F32)).astype(BF16)
    return dot(high, values) + dot(low, values)


def kernel(
    n_inst,
    n_mp,
    migrants,
    kv_heads,
    table_h,
    length_h,
    dest_h,
    local_h,
    slot_h,
    hidden,
    weight,
    gain,
    queries,
    pool,
    out,
    pool_v,
    hidden_v,
    weight_v,
    gain_v,
    query_v,
    stage,
    leaving,
    cache,
    part_out,
    part_in,
    key_all,
    value_all,
    table,
    length,
    mig_dest,
    mig_local,
    mig_slot,
    int_sem,
    in_sem,
    weight_sem,
    own_sem,
    page_send,
    page_recv,
    mig_send,
    mig_recv,
    part_send,
    part_recv,
):
    inst = lax.axis_index("inst")
    mp = lax.axis_index("mp")
    steps, requests, _ = hidden.shape
    head_dim = gain.shape[1]
    pair = 2 * head_dim
    page = pool.shape[1]
    rows = steps * requests
    portion = query_v.shape[2] // head_dim
    share = n_mp // kv_heads
    context = n_mp * page
    own_head = mp // share

    def columns(head):
        return pl.ds(pl.multiple_of(head * pair, pair), pair)

    loads = [
        pltpu.make_async_copy(pool, pool_v, in_sem.at[0]),
        pltpu.make_async_copy(hidden, hidden_v, in_sem.at[1]),
        pltpu.make_async_copy(
            queries.at[
                :,
                :,
                pl.ds(pl.multiple_of(mp * (portion * head_dim), head_dim), portion * head_dim),
            ],
            query_v,
            in_sem.at[2],
        ),
        pltpu.make_async_copy(gain, gain_v, in_sem.at[3]),
    ]
    heads = [lax.rem(own_head + 1 + j, kv_heads) for j in range(kv_heads)]
    weight_loads = [
        pltpu.make_async_copy(weight.at[:, columns(head)], weight_v.at[j], weight_sem.at[j])
        for j, head in enumerate(heads)
    ]
    int_loads = [
        pltpu.make_async_copy(source, target, int_sem.at[n])
        for n, (source, target) in enumerate(
            [
                (table_h, table),
                (slot_h, mig_slot),
                (dest_h, mig_dest),
                (local_h, mig_local),
                (length_h, length),
            ]
        )
    ]
    loads[0].start()
    for load in int_loads:
        load.start()
    loads[1].start()
    for load in weight_loads:
        load.start()
    loads[2].start()
    loads[3].start()

    barrier = pltpu.get_barrier_semaphore()

    def greet_instance(away, to_inst):
        def greet(other):
            pl.semaphore_signal(
                barrier, inc=1, device_id={"inst": to_inst, "mp": other}, device_id_type=MESH
            )

        loop(n_mp, greet)

    def greet_peer(k):
        pl.semaphore_signal(
            barrier,
            inc=1,
            device_id={"inst": inst, "mp": lax.rem(mp + 1 + k, n_mp)},
            device_id_type=MESH,
        )

    loop(n_mp - 1, greet_peer)
    loop(n_inst - 1, lambda k: greet_instance(k, lax.rem(inst + 1 + k, n_inst)))

    for load in int_loads:
        load.wait()
    loads[0].wait()
    for r in range(requests):
        stage[r] = pool_v[table[r]]

    def take_leaving(k):
        to_inst = lax.rem(inst + 1 + k, n_inst)
        slot = mig_slot[0]
        for u in range(1, migrants):
            slot = jnp.where(mig_dest[u, inst] == to_inst, mig_slot[u], slot)
        leaving[k] = pool_v[slot]

    loop(n_inst - 1, take_leaving)

    def page_copy(k):
        to = lax.rem(mp + 1 + k, n_mp)
        return pltpu.make_async_remote_copy(
            src_ref=stage.at[:, :, columns(to // share)],
            dst_ref=cache.at[pl.ds(0, requests), mp],
            send_sem=page_send.at[k],
            recv_sem=page_recv.at[k],
            device_id={"inst": inst, "mp": to},
            device_id_type=MESH,
        )

    def mig_copy(k, to, column):
        return pltpu.make_async_remote_copy(
            src_ref=leaving.at[k, :, columns(to // share)],
            dst_ref=cache.at[requests + k, column],
            send_sem=mig_send.at[k, to],
            recv_sem=mig_recv.at[k, column],
            device_id={"inst": lax.rem(inst + 1 + k, n_inst), "mp": to},
            device_id_type=MESH,
        )

    def part_copy(j, k):
        to = lax.rem(mp + 1 + k, n_mp)
        return pltpu.make_async_remote_copy(
            src_ref=part_out.at[j],
            dst_ref=part_in.at[k],
            send_sem=part_send.at[k],
            recv_sem=part_recv.at[k],
            device_id={"inst": inst, "mp": to},
            device_id_type=MESH,
        )

    own_copy = pltpu.make_async_copy(
        stage.at[:, :, columns(own_head)], cache.at[pl.ds(0, requests), mp], own_sem
    )
    own_copy.start()

    pl.semaphore_wait(barrier, n_inst * n_mp - 1)
    loop(n_mp - 1, lambda k: page_copy(k).start())
    loop(n_inst - 1, lambda k: loop(n_mp, lambda to: mig_copy(k, to, mp).start()))

    loads[1].wait()
    features = hidden_v[...].astype(F32).reshape(rows, hidden.shape[2]).astype(BF16)
    for j in range(kv_heads):
        weight_loads[j].wait()
        part_out[j] = dot(features, weight_v[j])
        if share == 1:
            if j < kv_heads - 1:
                part_copy(j, j).start()
    if share > 1:

        def send_part(k):
            to = lax.rem(mp + 1 + k, n_mp)
            j = lax.rem(to // share - own_head - 1 + 2 * kv_heads, kv_heads)
            part_copy(j, k).start()

        loop(n_mp - 1, send_part)

    block = [jnp.int32(r) for r in range(requests)]
    for k in range(n_inst - 1):
        source = lax.rem(inst + 2 * n_inst - 1 - k, n_inst)
        place = jnp.int32(-1)
        for u in range(migrants):
            place = jnp.where(mig_dest[u, source] == inst, mig_local[u, source], place)
        for r in range(requests):
            block[r] = jnp.where(place == r, requests + k, block[r])

    row8 = lax.broadcasted_iota(jnp.int32, (requests, head_dim), 0)
    length8 = jnp.zeros((requests, head_dim), jnp.int32)
    for r in range(requests):
        length8 = jnp.where(row8 == r, length[r], length8)

    half = head_dim // 2
    lane = lax.broadcasted_iota(jnp.int32, (rows, head_dim), 1)
    pair_index = jnp.where(lane < half, lane, lane - half)
    frequency = jnp.exp(-(2.0 * pair_index.astype(F32) / head_dim) * math.log(1000000.0))
    place = jnp.concatenate([(length8 + t).astype(F32) for t in range(steps)], axis=0)
    angle = place * frequency
    cosine = jnp.cos(angle)
    sine = jnp.sin(angle)
    sine = jnp.where(lane < half, -sine, sine)

    cached_lane = lax.broadcasted_iota(jnp.int32, (requests, requests * context), 1)
    first = lax.broadcasted_iota(jnp.int32, (requests, requests * context), 0) * context
    last = first + jnp.broadcast_to(length8[:, :1], first.shape)
    bias = jnp.where((cached_lane >= first) & (cached_lane < last), 0.0, -1e30).astype(F32)

    row = lax.broadcasted_iota(jnp.int32, (rows, 128), 0)
    column = lax.broadcasted_iota(jnp.int32, (rows, 128), 1)
    fresh_bias = jnp.where(
        (lax.rem(row, requests) == lax.rem(column, requests)) & (column <= row), 0.0, -1e30
    ).astype(F32)

    loads[2].wait()
    query = jnp.concatenate(
        [
            query_v[t, :, g * head_dim : (g + 1) * head_dim].astype(F32)
            for g in range(portion)
            for t in range(steps)
        ],
        axis=0,
    ).astype(BF16)
    value_all[:, head_dim:] = jnp.ones((requests * context, head_dim), BF16)
    scale = 1.0 / math.sqrt(head_dim)

    own_copy.wait()
    loop(n_mp - 1, lambda k: page_copy(k).wait_recv())
    loop(n_inst - 1, lambda k: loop(n_mp, lambda to: mig_copy(k, to, to).wait_recv()))
    for r in range(requests):
        held = cache[block[r]].reshape(context, pair)
        key_all[r * context : (r + 1) * context, :] = held[:, :head_dim]
        value_all[r * context : (r + 1) * context, :head_dim] = held[:, head_dim:]

    total_rows = portion * rows
    scores = dot(query, key_all[...], ((1,), (1,))) * scale
    scores = scores.reshape(portion * steps, requests, requests * context) + bias[None]
    scores = scores.reshape(total_rows, requests * context)
    peak = jnp.max(scores, axis=-1, keepdims=True)
    summed = weighted(jnp.exp(scores - peak), value_all[...])

    loads[3].wait()
    loop(n_mp - 1, lambda k: part_copy(0, k).wait_recv())
    projected = part_out[kv_heads - 1]
    for k in range(n_mp - 1):
        projected = projected + part_in[k]
    keys = projected[:, :head_dim]
    factor = lax.rsqrt(jnp.mean(keys * keys, axis=-1, keepdims=True) + 1e-06)
    keys = keys * factor * gain_v[...]
    keys = keys * cosine + pltpu.roll(keys, half, 1) * sine
    blank = jnp.zeros((128 - rows, head_dim), F32)
    fresh_keys = jnp.concatenate([keys, blank], axis=0).astype(BF16)
    fresh_values = jnp.concatenate([projected[:, head_dim:], blank], axis=0).astype(BF16)
    fresh_values = jnp.concatenate(
        [fresh_values, jnp.ones((128, head_dim), BF16)], axis=1
    )
    fresh = dot(query, fresh_keys, ((1,), (1,))) * scale
    fresh = (fresh.reshape(portion, rows, 128) + fresh_bias[None]).reshape(total_rows, 128)
    highest = jnp.maximum(peak, jnp.max(fresh, axis=-1, keepdims=True))
    summed = summed * jnp.exp(peak - highest) + weighted(jnp.exp(fresh - highest), fresh_values)
    result = summed[:, :head_dim] / summed[:, head_dim:]
    for t in range(steps):
        for g in range(portion):
            at = (g * steps + t) * requests
            out[t, :, g * head_dim : (g + 1) * head_dim] = result[at : at + requests].astype(BF16)

    loop(n_mp - 1, lambda k: page_copy(k).wait_send())
    loop(n_inst - 1, lambda k: loop(n_mp, lambda to: mig_copy(k, to, mp).wait_send()))
    loop(n_mp - 1, lambda k: part_copy(0, k).wait_send())


def local(
    n_inst,
    n_mp,
    hidden_states,
    kv_weight,
    key_gain,
    queries,
    kv_pool,
    page_table,
    lengths,
    mig_dest,
    mig_local,
    mig_slots,
):
    steps, requests, depth = hidden_states.shape
    head_dim = key_gain.shape[0]
    width = kv_weight.shape[1]
    pair = 2 * head_dim
    kv_heads = width // pair
    portion = queries.shape[2] // n_mp
    migrants = mig_dest.shape[1]
    pool = kv_pool[0]
    page = pool.shape[1]
    rows = steps * requests
    context = n_mp * page
    assert page_table.shape[1] == 1 and n_mp % kv_heads == 0
    far = pl.BlockSpec(memory_space=pltpu.HBM)
    return pl.pallas_call(
        functools.partial(kernel, n_inst, n_mp, migrants, kv_heads),
        out_shape=jax.ShapeDtypeStruct((steps, requests, portion), BF16),
        in_specs=[far] * 10,
        out_specs=pl.BlockSpec(memory_space=pltpu.VMEM),
        scratch_shapes=[
            pltpu.VMEM(pool.shape, BF16),
            pltpu.VMEM(hidden_states.shape, BF16),
            pltpu.VMEM((kv_heads, depth, pair), BF16),
            pltpu.VMEM((1, head_dim), F32),
            pltpu.VMEM((steps, requests, portion), BF16),
            pltpu.VMEM((requests, page, width), BF16),
            pltpu.VMEM((n_inst - 1, page, width), BF16),
            pltpu.VMEM((requests + n_inst - 1, n_mp, page, pair), BF16),
            pltpu.VMEM((kv_heads, rows, pair), F32),
            pltpu.VMEM((n_mp - 1, rows, pair), F32),
            pltpu.VMEM((requests * context, head_dim), BF16),
            pltpu.VMEM((requests * context, pair), BF16),
            pltpu.SMEM((requests,), jnp.int32),
            pltpu.SMEM((requests,), jnp.int32),
            pltpu.SMEM((migrants, n_inst), jnp.int32),
            pltpu.SMEM((migrants, n_inst), jnp.int32),
            pltpu.SMEM((migrants,), jnp.int32),
            pltpu.SemaphoreType.DMA((5,)),
            pltpu.SemaphoreType.DMA((4,)),
            pltpu.SemaphoreType.DMA((kv_heads,)),
            pltpu.SemaphoreType.DMA,
            pltpu.SemaphoreType.DMA((n_mp - 1,)),
            pltpu.SemaphoreType.DMA((n_mp - 1,)),
            pltpu.SemaphoreType.DMA((n_inst - 1, n_mp)),
            pltpu.SemaphoreType.DMA((n_inst - 1, n_mp)),
            pltpu.SemaphoreType.DMA((n_mp - 1,)),
            pltpu.SemaphoreType.DMA((n_mp - 1,)),
        ],
        compiler_params=pltpu.CompilerParams(
            collective_id=0, has_side_effects=True, vmem_limit_bytes=60 * 1024 * 1024
        ),
    )(
        page_table.reshape(-1),
        lengths,
        mig_dest.T,
        mig_local.T,
        mig_slots.reshape(-1),
        hidden_states,
        kv_weight,
        key_gain.reshape(1, head_dim),
        queries,
        pool,
    )


def solution(mesh):
    placed = (
        P(None, ("groups", "inst"), "mp"),
        P("mp", None),
        P(),
        P(None, ("groups", "inst"), None),
        P(("groups", "inst"), "mp", None, None),
        P(("groups", "inst"), None, "mp"),
        P(("groups", "inst")),
        P("groups", None),
        P("groups", None),
        P(("groups", "inst"), None, None, "mp"),
    )
    return jax.shard_map(
        functools.partial(local, mesh.shape["inst"], mesh.shape["mp"]),
        mesh=mesh,
        in_specs=placed,
        out_specs=P(None, ("groups", "inst"), "mp"),
        check_vma=False,
    )
```

```python
import functools
import math

import jax
import jax.numpy as jnp
from jax import lax
from jax.experimental import pallas as pl
from jax.experimental.pallas import tpu as pltpu
from jax.sharding import PartitionSpec as P

MESH = pl.DeviceIdType.MESH
F32 = jnp.float32
BF16 = jnp.bfloat16


def loop(count, step):
    if count <= 4:
        for index in range(count):
            step(index)
    else:
        lax.fori_loop(0, count, lambda index, carry: (step(index), carry)[1], 0)


def dot(left, right, contract=((1,), (0,))):
    return lax.dot_general(left, right, (contract, ((), ())), preferred_element_type=F32)


def weighted(weights, values):
    high = weights.astype(BF16)
    low = (weights - high.astype(F32)).astype(BF16)
    return dot(high, values) + dot(low, values)


def kernel(
    n_inst,
    n_mp,
    migrants,
    kv_heads,
    table_h,
    length_h,
    dest_h,
    local_h,
    slot_h,
    hidden,
    weight,
    gain,
    queries,
    pool,
    out,
    pool_v,
    hidden_v,
    weight_v,
    gain_v,
    query_v,
    stage,
    leaving,
    cache,
    part_out,
    part_in,
    key_all,
    value_all,
    table,
    length,
    mig_dest,
    mig_local,
    mig_slot,
    int_sem,
    in_sem,
    weight_sem,
    own_sem,
    page_send,
    page_recv,
    mig_send,
    mig_recv,
    part_send,
    part_recv,
):
    inst = lax.axis_index("inst")
    mp = lax.axis_index("mp")
    steps, requests, _ = hidden.shape
    head_dim = gain.shape[1]
    pair = 2 * head_dim
    page = pool.shape[1]
    rows = steps * requests
    portion = query_v.shape[2] // head_dim
    share = n_mp // kv_heads
    context = n_mp * page
    own_head = mp // share

    def columns(head):
        return pl.ds(pl.multiple_of(head * pair, pair), pair)

    loads = [
        pltpu.make_async_copy(pool, pool_v, in_sem.at[0]),
        pltpu.make_async_copy(hidden, hidden_v, in_sem.at[1]),
        pltpu.make_async_copy(
            queries.at[
                :,
                :,
                pl.ds(pl.multiple_of(mp * (portion * head_dim), head_dim), portion * head_dim),
            ],
            query_v,
            in_sem.at[2],
        ),
        pltpu.make_async_copy(gain, gain_v, in_sem.at[3]),
    ]
    heads = [lax.rem(own_head + 1 + j, kv_heads) for j in range(kv_heads)]
    weight_loads = [
        pltpu.make_async_copy(weight.at[:, columns(head)], weight_v.at[j], weight_sem.at[j])
        for j, head in enumerate(heads)
    ]
    int_loads = [
        pltpu.make_async_copy(source, target, int_sem.at[n])
        for n, (source, target) in enumerate(
            [
                (table_h, table),
                (slot_h, mig_slot),
                (dest_h, mig_dest),
                (local_h, mig_local),
                (length_h, length),
            ]
        )
    ]
    loads[0].start()
    for load in int_loads:
        load.start()
    loads[1].start()
    for load in weight_loads:
        load.start()
    loads[2].start()
    loads[3].start()

    barrier = pltpu.get_barrier_semaphore()

    def greet_instance(away, to_inst):
        def greet(other):
            pl.semaphore_signal(
                barrier, inc=1, device_id={"inst": to_inst, "mp": other}, device_id_type=MESH
            )

        loop(n_mp, greet)

    def greet_peer(k):
        pl.semaphore_signal(
            barrier,
            inc=1,
            device_id={"inst": inst, "mp": lax.rem(mp + 1 + k, n_mp)},
            device_id_type=MESH,
        )

    loop(n_mp - 1, greet_peer)
    loop(n_inst - 1, lambda k: greet_instance(k, lax.rem(inst + 1 + k, n_inst)))

    for load in int_loads:
        load.wait()
    loads[0].wait()
    for r in range(requests):
        stage[r] = pool_v[table[r]]

    def take_leaving(k):
        to_inst = lax.rem(inst + 1 + k, n_inst)
        slot = mig_slot[0]
        for u in range(1, migrants):
            slot = jnp.where(mig_dest[u, inst] == to_inst, mig_slot[u], slot)
        leaving[k] = pool_v[slot]

    loop(n_inst - 1, take_leaving)

    def page_copy(k):
        to = lax.rem(mp + 1 + k, n_mp)
        return pltpu.make_async_remote_copy(
            src_ref=stage.at[:, :, columns(to // share)],
            dst_ref=cache.at[pl.ds(0, requests), mp],
            send_sem=page_send.at[k],
            recv_sem=page_recv.at[k],
            device_id={"inst": inst, "mp": to},
            device_id_type=MESH,
        )

    def mig_copy(k, to, column):
        return pltpu.make_async_remote_copy(
            src_ref=leaving.at[k, :, columns(to // share)],
            dst_ref=cache.at[requests + k, column],
            send_sem=mig_send.at[k, to],
            recv_sem=mig_recv.at[k, column],
            device_id={"inst": lax.rem(inst + 1 + k, n_inst), "mp": to},
            device_id_type=MESH,
        )

    def part_copy(j, k):
        to = lax.rem(mp + 1 + k, n_mp)
        return pltpu.make_async_remote_copy(
            src_ref=part_out.at[j],
            dst_ref=part_in.at[k],
            send_sem=part_send.at[k],
            recv_sem=part_recv.at[k],
            device_id={"inst": inst, "mp": to},
            device_id_type=MESH,
        )

    own_copy = pltpu.make_async_copy(
        stage.at[:, :, columns(own_head)], cache.at[pl.ds(0, requests), mp], own_sem
    )
    own_copy.start()

    pl.semaphore_wait(barrier, n_inst * n_mp - 1)
    loop(n_mp - 1, lambda k: page_copy(k).start())
    loop(n_inst - 1, lambda k: loop(n_mp, lambda to: mig_copy(k, to, mp).start()))

    loads[1].wait()
    features = hidden_v[...].astype(F32).reshape(rows, hidden.shape[2]).astype(BF16)
    for j in range(kv_heads):
        weight_loads[j].wait()
        part_out[j] = dot(features, weight_v[j])
        if share == 1:
            if j < kv_heads - 1:
                part_copy(j, j).start()
    if share > 1:

        def send_part(k):
            to = lax.rem(mp + 1 + k, n_mp)
            j = lax.rem(to // share - own_head - 1 + 2 * kv_heads, kv_heads)
            part_copy(j, k).start()

        loop(n_mp - 1, send_part)

    block = [jnp.int32(r) for r in range(requests)]
    for k in range(n_inst - 1):
        source = lax.rem(inst + 2 * n_inst - 1 - k, n_inst)
        place = jnp.int32(-1)
        for u in range(migrants):
            place = jnp.where(mig_dest[u, source] == inst, mig_local[u, source], place)
        for r in range(requests):
            block[r] = jnp.where(place == r, requests + k, block[r])

    row8 = lax.broadcasted_iota(jnp.int32, (requests, head_dim), 0)
    length8 = jnp.zeros((requests, head_dim), jnp.int32)
    for r in range(requests):
        length8 = jnp.where(row8 == r, length[r], length8)

    half = head_dim // 2
    lane = lax.broadcasted_iota(jnp.int32, (rows, head_dim), 1)
    pair_index = jnp.where(lane < half, lane, lane - half)
    frequency = jnp.exp(-(2.0 * pair_index.astype(F32) / head_dim) * math.log(1000000.0))
    place = jnp.concatenate([(length8 + t).astype(F32) for t in range(steps)], axis=0)
    angle = place * frequency
    cosine = jnp.cos(angle)
    sine = jnp.sin(angle)
    sine = jnp.where(lane < half, -sine, sine)

    cached_lane = lax.broadcasted_iota(jnp.int32, (requests, requests * context), 1)
    first = lax.broadcasted_iota(jnp.int32, (requests, requests * context), 0) * context
    last = first + jnp.broadcast_to(length8[:, :1], first.shape)
    bias = jnp.where((cached_lane >= first) & (cached_lane < last), 0.0, -1e30).astype(F32)

    row = lax.broadcasted_iota(jnp.int32, (rows, 128), 0)
    column = lax.broadcasted_iota(jnp.int32, (rows, 128), 1)
    fresh_bias = jnp.where(
        (lax.rem(row, requests) == lax.rem(column, requests)) & (column <= row), 0.0, -1e30
    ).astype(F32)

    loads[2].wait()
    query = jnp.concatenate(
        [
            query_v[t, :, g * head_dim : (g + 1) * head_dim].astype(F32)
            for g in range(portion)
            for t in range(steps)
        ],
        axis=0,
    ).astype(BF16)
    value_all[:, head_dim:] = jnp.ones((requests * context, head_dim), BF16)
    scale = 1.0 / math.sqrt(head_dim)

    own_copy.wait()
    loop(n_mp - 1, lambda k: page_copy(k).wait_recv())
    loop(n_inst - 1, lambda k: loop(n_mp, lambda to: mig_copy(k, to, to).wait_recv()))
    for r in range(requests):
        held = cache[block[r]].reshape(context, pair)
        key_all[r * context : (r + 1) * context, :] = held[:, :head_dim]
        value_all[r * context : (r + 1) * context, :head_dim] = held[:, head_dim:]

    total_rows = portion * rows
    scores = dot(query, key_all[...], ((1,), (1,))) * scale
    scores = scores.reshape(portion * steps, requests, requests * context) + bias[None]
    scores = scores.reshape(total_rows, requests * context)
    peak = jnp.max(scores, axis=-1, keepdims=True)
    summed = weighted(jnp.exp(scores - peak), value_all[...])

    loads[3].wait()
    loop(n_mp - 1, lambda k: part_copy(0, k).wait_recv())
    projected = part_out[kv_heads - 1]
    for k in range(n_mp - 1):
        projected = projected + part_in[k]
    keys = projected[:, :head_dim]
    factor = lax.rsqrt(jnp.mean(keys * keys, axis=-1, keepdims=True) + 1e-06)
    keys = keys * factor * gain_v[...]
    keys = keys * cosine + pltpu.roll(keys, half, 1) * sine
    blank = jnp.zeros((128 - rows, head_dim), F32)
    fresh_keys = jnp.concatenate([keys, blank], axis=0).astype(BF16)
    fresh_values = jnp.concatenate([projected[:, head_dim:], blank], axis=0).astype(BF16)
    fresh_values = jnp.concatenate(
        [fresh_values, jnp.ones((128, head_dim), BF16)], axis=1
    )
    fresh = dot(query, fresh_keys, ((1,), (1,))) * scale
    fresh = (fresh.reshape(portion, rows, 128) + fresh_bias[None]).reshape(total_rows, 128)
    highest = jnp.maximum(peak, jnp.max(fresh, axis=-1, keepdims=True))
    summed = summed * jnp.exp(peak - highest) + weighted(jnp.exp(fresh - highest), fresh_values)
    result = summed[:, :head_dim] / summed[:, head_dim:]
    for t in range(steps):
        for g in range(portion):
            at = (g * steps + t) * requests
            out[t, :, g * head_dim : (g + 1) * head_dim] = result[at : at + requests].astype(BF16)

    loop(n_mp - 1, lambda k: page_copy(k).wait_send())
    loop(n_inst - 1, lambda k: loop(n_mp, lambda to: mig_copy(k, to, mp).wait_send()))
    loop(n_mp - 1, lambda k: part_copy(0, k).wait_send())


def local(
    n_inst,
    n_mp,
    hidden_states,
    kv_weight,
    key_gain,
    queries,
    kv_pool,
    page_table,
    lengths,
    mig_dest,
    mig_local,
    mig_slots,
):
    steps, requests, depth = hidden_states.shape
    head_dim = key_gain.shape[0]
    width = kv_weight.shape[1]
    pair = 2 * head_dim
    kv_heads = width // pair
    portion = queries.shape[2] // n_mp
    migrants = mig_dest.shape[1]
    pool = kv_pool[0]
    page = pool.shape[1]
    rows = steps * requests
    context = n_mp * page
    assert page_table.shape[1] == 1 and n_mp % kv_heads == 0
    far = pl.BlockSpec(memory_space=pltpu.HBM)
    return pl.pallas_call(
        functools.partial(kernel, n_inst, n_mp, migrants, kv_heads),
        out_shape=jax.ShapeDtypeStruct((steps, requests, portion), BF16),
        in_specs=[far] * 10,
        out_specs=pl.BlockSpec(memory_space=pltpu.VMEM),
        scratch_shapes=[
            pltpu.VMEM(pool.shape, BF16),
            pltpu.VMEM(hidden_states.shape, BF16),
            pltpu.VMEM((kv_heads, depth, pair), BF16),
            pltpu.VMEM((1, head_dim), F32),
            pltpu.VMEM((steps, requests, portion), BF16),
            pltpu.VMEM((requests, page, width), BF16),
            pltpu.VMEM((n_inst - 1, page, width), BF16),
            pltpu.VMEM((requests + n_inst - 1, n_mp, page, pair), BF16),
            pltpu.VMEM((kv_heads, rows, pair), F32),
            pltpu.VMEM((n_mp - 1, rows, pair), F32),
            pltpu.VMEM((requests * context, head_dim), BF16),
            pltpu.VMEM((requests * context, pair), BF16),
            pltpu.SMEM((requests,), jnp.int32),
            pltpu.SMEM((requests,), jnp.int32),
            pltpu.SMEM((migrants, n_inst), jnp.int32),
            pltpu.SMEM((migrants, n_inst), jnp.int32),
            pltpu.SMEM((migrants,), jnp.int32),
            pltpu.SemaphoreType.DMA((5,)),
            pltpu.SemaphoreType.DMA((4,)),
            pltpu.SemaphoreType.DMA((kv_heads,)),
            pltpu.SemaphoreType.DMA,
            pltpu.SemaphoreType.DMA((n_mp - 1,)),
            pltpu.SemaphoreType.DMA((n_mp - 1,)),
            pltpu.SemaphoreType.DMA((n_inst - 1, n_mp)),
            pltpu.SemaphoreType.DMA((n_inst - 1, n_mp)),
            pltpu.SemaphoreType.DMA((n_mp - 1,)),
            pltpu.SemaphoreType.DMA((n_mp - 1,)),
        ],
        compiler_params=pltpu.CompilerParams(
            collective_id=0, has_side_effects=True, vmem_limit_bytes=32 * 1024 * 1024
        ),
    )(
        *[
            pltpu.with_memory_space_constraint(operand, pltpu.HBM)
            for operand in (
                page_table.reshape(-1),
                lengths,
                mig_dest.T,
                mig_local.T,
                mig_slots.reshape(-1),
                hidden_states,
                kv_weight,
                key_gain.reshape(1, head_dim),
                queries,
                pool,
            )
        ]
    )


def solution(mesh):
    placed = (
        P(None, ("groups", "inst"), "mp"),
        P("mp", None),
        P(),
        P(None, ("groups", "inst"), None),
        P(("groups", "inst"), "mp", None, None),
        P(("groups", "inst"), None, "mp"),
        P(("groups", "inst")),
        P("groups", None),
        P("groups", None),
        P(("groups", "inst"), None, None, "mp"),
    )
    return jax.shard_map(
        functools.partial(local, mesh.shape["inst"], mesh.shape["mp"]),
        mesh=mesh,
        in_specs=placed,
        out_specs=P(None, ("groups", "inst"), "mp"),
        check_vma=False,
    )
```

```python
import functools
import math

import jax
import jax.numpy as jnp
from jax import lax
from jax.experimental import pallas as pl
from jax.experimental.pallas import tpu as pltpu
from jax.sharding import PartitionSpec as P

MESH = pl.DeviceIdType.MESH
F32 = jnp.float32
BF16 = jnp.bfloat16


def loop(count, step):
    if count <= 4:
        for index in range(count):
            step(index)
    else:
        lax.fori_loop(0, count, lambda index, carry: (step(index), carry)[1], 0)


def dot(left, right, contract=((1,), (0,))):
    return lax.dot_general(left, right, (contract, ((), ())), preferred_element_type=F32)


def weighted(weights, values):
    high = weights.astype(BF16)
    low = (weights - high.astype(F32)).astype(BF16)
    return dot(high, values) + dot(low, values)


def kernel(
    n_inst,
    n_mp,
    migrants,
    kv_heads,
    table_h,
    length_h,
    dest_h,
    local_h,
    slot_h,
    hidden,
    weight,
    gain,
    queries,
    pool,
    out,
    pool_v,
    hidden_v,
    weight_v,
    gain_v,
    query_v,
    stage,
    leaving,
    cache,
    outgoing,
    passing,
    arrived,
    part_out,
    part_in,
    table,
    length,
    mig_dest,
    mig_local,
    mig_slot,
    int_sem,
    in_sem,
    weight_sem,
    own_sem,
    page_send,
    page_recv,
    leave_send,
    leave_recv,
    hop_send,
    hop_recv,
    part_send,
    part_recv,
):
    inst = lax.axis_index("inst")
    mp = lax.axis_index("mp")
    steps, requests, _ = hidden.shape
    head_dim = gain.shape[1]
    pair = 2 * head_dim
    page = pool.shape[1]
    rows = steps * requests
    portion = query_v.shape[2] // head_dim
    share = n_mp // kv_heads
    context = n_mp * page
    own_head = mp // share

    def columns(head):
        return pl.ds(pl.multiple_of(head * pair, pair), pair)

    loads = [
        pltpu.make_async_copy(pool, pool_v, in_sem.at[0]),
        pltpu.make_async_copy(hidden, hidden_v, in_sem.at[1]),
        pltpu.make_async_copy(
            queries.at[
                :,
                :,
                pl.ds(pl.multiple_of(mp * (portion * head_dim), head_dim), portion * head_dim),
            ],
            query_v,
            in_sem.at[2],
        ),
        pltpu.make_async_copy(gain, gain_v, in_sem.at[3]),
    ]
    heads = [lax.rem(own_head + 1 + j, kv_heads) for j in range(kv_heads)]
    weight_loads = [
        pltpu.make_async_copy(weight.at[:, columns(head)], weight_v.at[j], weight_sem.at[j])
        for j, head in enumerate(heads)
    ]
    int_loads = [
        pltpu.make_async_copy(source, target, int_sem.at[n])
        for n, (source, target) in enumerate(
            [
                (table_h, table),
                (slot_h, mig_slot),
                (dest_h, mig_dest),
                (local_h, mig_local),
                (length_h, length),
            ]
        )
    ]
    loads[0].start()
    for load in int_loads:
        load.start()
    loads[1].start()
    for load in weight_loads:
        load.start()
    loads[2].start()
    loads[3].start()

    barrier = pltpu.get_barrier_semaphore()

    def greet_peer(k):
        pl.semaphore_signal(
            barrier,
            inc=1,
            device_id={"inst": inst, "mp": lax.rem(mp + 1 + k, n_mp)},
            device_id_type=MESH,
        )

    loop(n_mp - 1, greet_peer)
    for away, there in ((1, inst < n_inst - 1), (-1, inst > 0)):

        @pl.when(there)
        def _():
            pl.semaphore_signal(
                barrier, inc=1, device_id={"inst": inst + away, "mp": mp}, device_id_type=MESH
            )

    greetings = (
        n_mp - 1 + jnp.where(inst < n_inst - 1, 1, 0) + jnp.where(inst > 0, 1, 0)
    )

    for load in int_loads:
        load.wait()
    loads[0].wait()
    for r in range(requests):
        stage[r] = pool_v[table[r]]

    def take_leaving(k):
        to_inst = jnp.where(k < inst, k, k + 1)
        slot = mig_slot[0]
        for u in range(1, migrants):
            slot = jnp.where(mig_dest[u, inst] == to_inst, mig_slot[u], slot)
        leaving[k] = pool_v[slot]

    loop(n_inst - 1, take_leaving)

    def page_copy(k):
        to = lax.rem(mp + 1 + k, n_mp)
        return pltpu.make_async_remote_copy(
            src_ref=stage.at[:, :, columns(to // share)],
            dst_ref=cache.at[pl.ds(0, requests), mp],
            send_sem=page_send.at[k],
            recv_sem=page_recv.at[k],
            device_id={"inst": inst, "mp": to},
            device_id_type=MESH,
        )

    def leave_copy(k):
        to = lax.rem(mp + 1 + k, n_mp)
        return pltpu.make_async_remote_copy(
            src_ref=leaving.at[:, :, columns(to // share)],
            dst_ref=outgoing.at[:, mp],
            send_sem=leave_send.at[k],
            recv_sem=leave_recv.at[k],
            device_id={"inst": inst, "mp": to},
            device_id_type=MESH,
        )

    def line(way):
        return inst if way == 0 else n_inst - 1 - inst

    def sends(way, hop, rest):
        return (line(way) >= hop - 1) & (line(way) + rest <= n_inst - 1)

    def receives(way, hop, rest):
        return (line(way) >= hop) & (line(way) + rest <= n_inst)

    def hop_target(way, at, hop, rest):
        source = at - hop
        if rest == 1:
            return arrived.at[source if way == 0 else n_inst - 2 - source]
        return passing.at[way, source * (n_inst - 1 - at) + rest - 2]

    def hop_copy(way, hop, rest):
        at = line(way)
        if hop == 1:
            target = at + rest
            source = outgoing.at[target - 1 if way == 0 else n_inst - 1 - target]
        else:
            source = passing.at[way, (at - hop + 1) * (n_inst - 1 - at) + rest - 1]
        return pltpu.make_async_remote_copy(
            src_ref=source,
            dst_ref=hop_target(way, at + 1, hop, rest),
            send_sem=hop_send.at[way, hop - 1, rest - 1],
            recv_sem=hop_recv.at[way, hop - 1, rest - 1],
            device_id={"inst": inst + 1 - 2 * way, "mp": mp},
            device_id_type=MESH,
        )

    def hop_wait(way, hop, rest):
        @pl.when(receives(way, hop, rest))
        def _():
            target = hop_target(way, line(way), hop, rest)
            pltpu.make_async_remote_copy(
                src_ref=outgoing.at[0],
                dst_ref=target,
                send_sem=hop_send.at[way, hop - 1, rest - 1],
                recv_sem=hop_recv.at[way, hop - 1, rest - 1],
                device_id={"inst": inst + 1 - 2 * way, "mp": mp},
                device_id_type=MESH,
            ).wait_recv()

    def hop_start(hop):
        for rest in range(n_inst - hop, 0, -1):
            for way in range(2):
                if hop > 1:
                    hop_wait(way, hop - 1, rest + 1)

                @pl.when(sends(way, hop, rest))
                def _():
                    hop_copy(way, hop, rest).start()

    def part_copy(j, k):
        to = lax.rem(mp + 1 + k, n_mp)
        return pltpu.make_async_remote_copy(
            src_ref=part_out.at[j],
            dst_ref=part_in.at[k],
            send_sem=part_send.at[k],
            recv_sem=part_recv.at[k],
            device_id={"inst": inst, "mp": to},
            device_id_type=MESH,
        )

    own_copies = [
        pltpu.make_async_copy(
            stage.at[:, :, columns(own_head)], cache.at[pl.ds(0, requests), mp], own_sem.at[0]
        ),
        pltpu.make_async_copy(
            leaving.at[:, :, columns(own_head)], outgoing.at[:, mp], own_sem.at[1]
        ),
    ]
    for copy in own_copies:
        copy.start()

    pl.semaphore_wait(barrier, greetings)
    loop(n_mp - 1, lambda k: leave_copy(k).start())
    loop(n_mp - 1, lambda k: page_copy(k).start())

    loads[1].wait()
    features = hidden_v[...].astype(F32).reshape(rows, hidden.shape[2]).astype(BF16)
    for j in range(kv_heads):
        weight_loads[j].wait()
        part_out[j] = dot(features, weight_v[j])
        if share == 1:
            if j < kv_heads - 1:
                part_copy(j, j).start()
    if share > 1:

        def send_part(k):
            to = lax.rem(mp + 1 + k, n_mp)
            j = lax.rem(to // share - own_head - 1 + 2 * kv_heads, kv_heads)
            part_copy(j, k).start()

        loop(n_mp - 1, send_part)

    count = jnp.int32(0)
    place = [jnp.int32(0)] * migrants
    guest = [jnp.int32(-1)] * migrants
    for k in range(n_inst - 1):
        source = jnp.where(k < inst, k, k + 1)
        for u in range(migrants):
            here = mig_dest[u, source] == inst
            for v in range(migrants):
                hit = here & (count == v)
                place[v] = jnp.where(hit, k, place[v])
                guest[v] = jnp.where(hit, mig_local[u, source], guest[v])
            count = count + jnp.where(here, 1, 0)

    row8 = lax.broadcasted_iota(jnp.int32, (requests, head_dim), 0)
    length8 = jnp.zeros((requests, head_dim), jnp.int32)
    for r in range(requests):
        length8 = jnp.where(row8 == r, length[r], length8)

    half = head_dim // 2
    lane = lax.broadcasted_iota(jnp.int32, (rows, head_dim), 1)
    pair_index = jnp.where(lane < half, lane, lane - half)
    frequency = jnp.exp(-(2.0 * pair_index.astype(F32) / head_dim) * math.log(1000000.0))
    position = jnp.concatenate([(length8 + t).astype(F32) for t in range(steps)], axis=0)
    angle = position * frequency
    cosine = jnp.cos(angle)
    sine = jnp.sin(angle)
    sine = jnp.where(lane < half, -sine, sine)

    stay8 = length8
    for v in range(migrants):
        stay8 = jnp.where(row8 == guest[v], 0, stay8)
    cached_lane = lax.broadcasted_iota(jnp.int32, (requests, requests * context), 1)
    first = lax.broadcasted_iota(jnp.int32, (requests, requests * context), 0) * context
    last = first + jnp.broadcast_to(stay8[:, :1], first.shape)
    bias = jnp.where((cached_lane >= first) & (cached_lane < last), 0.0, -1e30).astype(F32)

    guests = migrants * context
    guest_lane = lax.broadcasted_iota(jnp.int32, (requests, guests), 1)
    guest_row = lax.broadcasted_iota(jnp.int32, (requests, guests), 0)
    guest_length = jnp.broadcast_to(length8[:, :1], guest_lane.shape)
    known = guest_row < 0
    for v in range(migrants):
        known = known | (
            (guest_row == guest[v])
            & (guest_lane >= v * context)
            & (guest_lane < v * context + guest_length)
        )
    guest_bias = jnp.where(known, 0.0, -1e30).astype(F32)
    row = lax.broadcasted_iota(jnp.int32, (rows, 128), 0)
    column = lax.broadcasted_iota(jnp.int32, (rows, 128), 1)
    fresh_bias = jnp.where(
        (lax.rem(row, requests) == lax.rem(column, requests)) & (column <= row), 0.0, -1e30
    ).astype(F32)
    late_bias = jnp.concatenate(
        [jnp.concatenate([guest_bias] * steps, axis=0), fresh_bias], axis=1
    )

    loads[2].wait()
    query = jnp.concatenate(
        [
            query_v[t, :, g * head_dim : (g + 1) * head_dim].astype(F32)
            for g in range(portion)
            for t in range(steps)
        ],
        axis=0,
    ).astype(BF16)
    scale = 1.0 / math.sqrt(head_dim)

    def with_ones(values):
        return jnp.concatenate([values, jnp.ones(values.shape, BF16)], axis=1)

    own_copies[1].wait()
    loop(n_mp - 1, lambda k: leave_copy(k).wait_recv())
    for hop in range(1, n_inst):
        hop_start(hop)

    own_copies[0].wait()
    loop(n_mp - 1, lambda k: page_copy(k).wait_recv())
    held = cache[...].reshape(requests * context, pair)
    total_rows = portion * rows
    scores = dot(query, held[:, :head_dim], ((1,), (1,))) * scale
    scores = scores.reshape(portion * steps, requests, requests * context) + bias[None]
    scores = scores.reshape(total_rows, requests * context)
    peak = jnp.max(scores, axis=-1, keepdims=True)
    summed = weighted(jnp.exp(scores - peak), with_ones(held[:, head_dim:]))

    loads[3].wait()
    loop(n_mp - 1, lambda k: part_copy(0, k).wait_recv())
    projected = part_out[kv_heads - 1]
    for k in range(n_mp - 1):
        projected = projected + part_in[k]
    keys = projected[:, :head_dim]
    factor = lax.rsqrt(jnp.mean(keys * keys, axis=-1, keepdims=True) + 1e-06)
    keys = keys * factor * gain_v[...]
    keys = keys * cosine + pltpu.roll(keys, half, 1) * sine
    blank = jnp.zeros((128 - rows, head_dim), F32)
    fresh_keys = jnp.concatenate([keys, blank], axis=0).astype(BF16)
    fresh_values = jnp.concatenate([projected[:, head_dim:], blank], axis=0).astype(BF16)

    for hop in range(1, n_inst):
        for way in range(2):
            hop_wait(way, hop, 1)
    came = [arrived[place[v]].reshape(context, pair) for v in range(migrants)]
    late_keys = jnp.concatenate([page[:, :head_dim] for page in came] + [fresh_keys], axis=0)
    late_values = jnp.concatenate([page[:, head_dim:] for page in came] + [fresh_values], axis=0)
    late = dot(query, late_keys, ((1,), (1,))) * scale
    late = (late.reshape(portion, rows, guests + 128) + late_bias[None]).reshape(
        total_rows, guests + 128
    )
    highest = jnp.maximum(peak, jnp.max(late, axis=-1, keepdims=True))
    summed = summed * jnp.exp(peak - highest) + weighted(
        jnp.exp(late - highest), with_ones(late_values)
    )
    result = summed[:, :head_dim] / summed[:, head_dim:]
    for t in range(steps):
        for g in range(portion):
            at = (g * steps + t) * requests
            out[t, :, g * head_dim : (g + 1) * head_dim] = result[at : at + requests].astype(BF16)

    loop(n_mp - 1, lambda k: page_copy(k).wait_send())
    loop(n_mp - 1, lambda k: leave_copy(k).wait_send())
    for hop in range(1, n_inst):
        for rest in range(n_inst - hop, 0, -1):
            for way in range(2):

                @pl.when(sends(way, hop, rest))
                def _():
                    hop_copy(way, hop, rest).wait_send()

    loop(n_mp - 1, lambda k: part_copy(0, k).wait_send())


def local(
    n_inst,
    n_mp,
    hidden_states,
    kv_weight,
    key_gain,
    queries,
    kv_pool,
    page_table,
    lengths,
    mig_dest,
    mig_local,
    mig_slots,
):
    steps, requests, depth = hidden_states.shape
    head_dim = key_gain.shape[0]
    width = kv_weight.shape[1]
    pair = 2 * head_dim
    kv_heads = width // pair
    portion = queries.shape[2] // n_mp
    migrants = mig_dest.shape[1]
    pool = kv_pool[0]
    page = pool.shape[1]
    rows = steps * requests
    assert page_table.shape[1] == 1 and n_mp % kv_heads == 0
    far = pl.BlockSpec(memory_space=pltpu.HBM)
    return pl.pallas_call(
        functools.partial(kernel, n_inst, n_mp, migrants, kv_heads),
        out_shape=jax.ShapeDtypeStruct((steps, requests, portion), BF16),
        in_specs=[far] * 10,
        out_specs=pl.BlockSpec(memory_space=pltpu.VMEM),
        scratch_shapes=[
            pltpu.VMEM(pool.shape, BF16),
            pltpu.VMEM(hidden_states.shape, BF16),
            pltpu.VMEM((kv_heads, depth, pair), BF16),
            pltpu.VMEM((1, head_dim), F32),
            pltpu.VMEM((steps, requests, portion), BF16),
            pltpu.VMEM((requests, page, width), BF16),
            pltpu.VMEM((n_inst - 1, page, width), BF16),
            pltpu.VMEM((requests, n_mp, page, pair), BF16),
            pltpu.VMEM((n_inst - 1, n_mp, page, pair), BF16),
            pltpu.VMEM((2, max(n_inst * n_inst // 4, 1), n_mp, page, pair), BF16),
            pltpu.VMEM((n_inst - 1, n_mp, page, pair), BF16),
            pltpu.VMEM((kv_heads, rows, pair), F32),
            pltpu.VMEM((n_mp - 1, rows, pair), F32),
            pltpu.SMEM((requests,), jnp.int32),
            pltpu.SMEM((requests,), jnp.int32),
            pltpu.SMEM((migrants, n_inst), jnp.int32),
            pltpu.SMEM((migrants, n_inst), jnp.int32),
            pltpu.SMEM((migrants,), jnp.int32),
            pltpu.SemaphoreType.DMA((5,)),
            pltpu.SemaphoreType.DMA((4,)),
            pltpu.SemaphoreType.DMA((kv_heads,)),
            pltpu.SemaphoreType.DMA((2,)),
            pltpu.SemaphoreType.DMA((n_mp - 1,)),
            pltpu.SemaphoreType.DMA((n_mp - 1,)),
            pltpu.SemaphoreType.DMA((n_mp - 1,)),
            pltpu.SemaphoreType.DMA((n_mp - 1,)),
            pltpu.SemaphoreType.DMA((2, n_inst - 1, n_inst - 1)),
            pltpu.SemaphoreType.DMA((2, n_inst - 1, n_inst - 1)),
            pltpu.SemaphoreType.DMA((n_mp - 1,)),
            pltpu.SemaphoreType.DMA((n_mp - 1,)),
        ],
        compiler_params=pltpu.CompilerParams(
            collective_id=0, has_side_effects=True, vmem_limit_bytes=32 * 1024 * 1024
        ),
    )(
        *[
            pltpu.with_memory_space_constraint(operand, pltpu.HBM)
            for operand in (
                page_table.reshape(-1),
                lengths,
                mig_dest.T,
                mig_local.T,
                mig_slots.reshape(-1),
                hidden_states,
                kv_weight,
                key_gain.reshape(1, head_dim),
                queries,
                pool,
            )
        ]
    )


def solution(mesh):
    placed = (
        P(None, ("groups", "inst"), "mp"),
        P("mp", None),
        P(),
        P(None, ("groups", "inst"), None),
        P(("groups", "inst"), "mp", None, None),
        P(("groups", "inst"), None, "mp"),
        P(("groups", "inst")),
        P("groups", None),
        P("groups", None),
        P(("groups", "inst"), None, None, "mp"),
    )
    return jax.shard_map(
        functools.partial(local, mesh.shape["inst"], mesh.shape["mp"]),
        mesh=mesh,
        in_specs=placed,
        out_specs=P(None, ("groups", "inst"), "mp"),
        check_vma=False,
    )
```

```python
import functools
import math

import jax
import jax.numpy as jnp
from jax import lax
from jax.experimental import pallas as pl
from jax.experimental.pallas import tpu as pltpu
from jax.sharding import PartitionSpec as P

MESH = pl.DeviceIdType.MESH
F32 = jnp.float32
BF16 = jnp.bfloat16


def loop(count, step):
    if count <= 4:
        for index in range(count):
            step(index)
    else:
        lax.fori_loop(0, count, lambda index, carry: (step(index), carry)[1], 0)


def dot(left, right, contract=((1,), (0,))):
    return lax.dot_general(left, right, (contract, ((), ())), preferred_element_type=F32)


def weighted(weights, values):
    high = weights.astype(BF16)
    low = (weights - high.astype(F32)).astype(BF16)
    return dot(high, values) + dot(low, values)


def kernel(
    n_inst,
    n_mp,
    migrants,
    kv_heads,
    table_h,
    length_h,
    dest_h,
    local_h,
    slot_h,
    hidden,
    weight,
    gain,
    queries,
    pool,
    out,
    pool_v,
    hidden_v,
    weight_v,
    gain_v,
    query_v,
    stage,
    leaving,
    cache,
    outgoing,
    moving,
    arrived,
    part_out,
    part_in,
    table,
    length,
    mig_dest,
    mig_local,
    mig_slot,
    int_sem,
    in_sem,
    weight_sem,
    own_sem,
    page_send,
    page_recv,
    leave_send,
    leave_recv,
    move_send,
    move_recv,
    news,
    part_send,
    part_recv,
):
    inst = lax.axis_index("inst")
    mp = lax.axis_index("mp")
    steps, requests, _ = hidden.shape
    head_dim = gain.shape[1]
    pair = 2 * head_dim
    page = pool.shape[1]
    rows = steps * requests
    portion = query_v.shape[2] // head_dim
    share = n_mp // kv_heads
    context = n_mp * page
    own_head = mp // share

    def columns(head):
        return pl.ds(pl.multiple_of(head * pair, pair), pair)

    loads = [
        pltpu.make_async_copy(pool, pool_v, in_sem.at[0]),
        pltpu.make_async_copy(hidden, hidden_v, in_sem.at[1]),
        pltpu.make_async_copy(
            queries.at[
                :,
                :,
                pl.ds(pl.multiple_of(mp * (portion * head_dim), head_dim), portion * head_dim),
            ],
            query_v,
            in_sem.at[2],
        ),
        pltpu.make_async_copy(gain, gain_v, in_sem.at[3]),
    ]
    heads = [lax.rem(own_head + 1 + j, kv_heads) for j in range(kv_heads)]
    weight_loads = [
        pltpu.make_async_copy(weight.at[:, columns(head)], weight_v.at[j], weight_sem.at[j])
        for j, head in enumerate(heads)
    ]
    int_loads = [
        pltpu.make_async_copy(source, target, int_sem.at[n])
        for n, (source, target) in enumerate(
            [
                (table_h, table),
                (slot_h, mig_slot),
                (dest_h, mig_dest),
                (local_h, mig_local),
                (length_h, length),
            ]
        )
    ]
    loads[0].start()
    for load in int_loads:
        load.start()
    loads[1].start()
    loads[2].start()
    loads[3].start()
    for load in weight_loads:
        load.start()

    barrier = pltpu.get_barrier_semaphore()

    def greet_peer(k):
        pl.semaphore_signal(
            barrier,
            inc=1,
            device_id={"inst": inst, "mp": lax.rem(mp + 1 + k, n_mp)},
            device_id_type=MESH,
        )

    loop(n_mp - 1, greet_peer)
    for away, there in ((1, inst < n_inst - 1), (-1, inst > 0)):

        @pl.when(there)
        def _():
            pl.semaphore_signal(
                barrier, inc=1, device_id={"inst": inst + away, "mp": mp}, device_id_type=MESH
            )

    greetings = (
        n_mp - 1 + jnp.where(inst < n_inst - 1, 1, 0) + jnp.where(inst > 0, 1, 0)
    )

    for load in int_loads:
        load.wait()
    loads[0].wait()
    for r in range(requests):
        stage[r] = pool_v[table[r]]

    for u in range(migrants):
        leaving[u] = pool_v[mig_slot[u]]

    def page_copy(k):
        to = lax.rem(mp + 1 + k, n_mp)
        return pltpu.make_async_remote_copy(
            src_ref=stage.at[:, :, columns(to // share)],
            dst_ref=cache.at[pl.ds(0, requests), mp],
            send_sem=page_send.at[k],
            recv_sem=page_recv.at[k],
            device_id={"inst": inst, "mp": to},
            device_id_type=MESH,
        )

    def leave_copy(k):
        to = lax.rem(mp + 1 + k, n_mp)
        return pltpu.make_async_remote_copy(
            src_ref=leaving.at[:, :, columns(to // share)],
            dst_ref=outgoing.at[:, mp],
            send_sem=leave_send.at[k],
            recv_sem=leave_recv.at[k],
            device_id={"inst": inst, "mp": to},
            device_id_type=MESH,
        )

    def move_copy(k):
        to = jnp.where(k < inst, k, k + 1)
        return pltpu.make_async_remote_copy(
            src_ref=moving.at[k],
            dst_ref=arrived.at[jnp.where(inst < to, inst, inst - 1)],
            send_sem=move_send.at[k],
            recv_sem=move_recv.at[jnp.where(inst < to, inst, inst - 1)],
            device_id={"inst": to, "mp": mp},
            device_id_type=MESH,
        )

    def move_wait(k):
        source = jnp.where(k < inst, k, k + 1)
        pltpu.make_async_remote_copy(
            src_ref=moving.at[k],
            dst_ref=arrived.at[k],
            send_sem=move_send.at[k],
            recv_sem=move_recv.at[k],
            device_id={"inst": source, "mp": mp},
            device_id_type=MESH,
        ).wait_recv()

    def line(way):
        return inst if way == 0 else n_inst - 1 - inst

    def tell(way, far):
        @pl.when((line(way) > 0) & (line(way) + far <= n_inst - 1))
        def _():
            pl.semaphore_signal(
                news.at[way, far - 1],
                inc=1,
                device_id={"inst": inst - 1 + 2 * way, "mp": mp},
                device_id_type=MESH,
            )

    def hear(far):
        for way in range(2):

            @pl.when(line(way) + 1 + far <= n_inst - 1)
            def _():
                pl.semaphore_wait(news.at[way, far - 1], 1)

            if far + 1 <= n_inst - 2:
                tell(way, far + 1)

    def part_copy(j, k):
        to = lax.rem(mp + 1 + k, n_mp)
        return pltpu.make_async_remote_copy(
            src_ref=part_out.at[j],
            dst_ref=part_in.at[k],
            send_sem=part_send.at[k],
            recv_sem=part_recv.at[k],
            device_id={"inst": inst, "mp": to},
            device_id_type=MESH,
        )

    own_copies = [
        pltpu.make_async_copy(
            stage.at[:, :, columns(own_head)], cache.at[pl.ds(0, requests), mp], own_sem.at[0]
        ),
        pltpu.make_async_copy(
            leaving.at[:, :, columns(own_head)], outgoing.at[:, mp], own_sem.at[1]
        ),
    ]
    for copy in own_copies:
        copy.start()

    count = jnp.int32(0)
    place = [jnp.int32(0)] * migrants
    guest = [jnp.int32(-1)] * migrants
    for k in range(n_inst - 1):
        source = jnp.where(k < inst, k, k + 1)
        for u in range(migrants):
            here = mig_dest[u, source] == inst
            for v in range(migrants):
                hit = here & (count == v)
                place[v] = jnp.where(hit, k, place[v])
                guest[v] = jnp.where(hit, mig_local[u, source], guest[v])
            count = count + jnp.where(here, 1, 0)

    row8 = lax.broadcasted_iota(jnp.int32, (requests, head_dim), 0)
    length8 = jnp.zeros((requests, head_dim), jnp.int32)
    for r in range(requests):
        length8 = jnp.where(row8 == r, length[r], length8)

    half = head_dim // 2
    lane = lax.broadcasted_iota(jnp.int32, (rows, head_dim), 1)
    pair_index = jnp.where(lane < half, lane, lane - half)
    frequency = jnp.exp(-(2.0 * pair_index.astype(F32) / head_dim) * math.log(1000000.0))
    position = jnp.concatenate([(length8 + t).astype(F32) for t in range(steps)], axis=0)
    angle = position * frequency
    cosine = jnp.cos(angle)
    sine = jnp.sin(angle)
    sine = jnp.where(lane < half, -sine, sine)

    stay8 = length8
    for v in range(migrants):
        stay8 = jnp.where(row8 == guest[v], 0, stay8)
    cached_lane = lax.broadcasted_iota(jnp.int32, (requests, requests * context), 1)
    first = lax.broadcasted_iota(jnp.int32, (requests, requests * context), 0) * context
    last = first + jnp.broadcast_to(stay8[:, :1], first.shape)
    bias = jnp.where((cached_lane >= first) & (cached_lane < last), 0.0, -1e30).astype(F32)

    guests = migrants * context
    guest_lane = lax.broadcasted_iota(jnp.int32, (requests, guests), 1)
    guest_row = lax.broadcasted_iota(jnp.int32, (requests, guests), 0)
    guest_length = jnp.broadcast_to(length8[:, :1], guest_lane.shape)
    known = guest_row < 0
    for v in range(migrants):
        known = known | (
            (guest_row == guest[v])
            & (guest_lane >= v * context)
            & (guest_lane < v * context + guest_length)
        )
    guest_bias = jnp.where(known, 0.0, -1e30).astype(F32)
    row = lax.broadcasted_iota(jnp.int32, (rows, 128), 0)
    column = lax.broadcasted_iota(jnp.int32, (rows, 128), 1)
    fresh_bias = jnp.where(
        (lax.rem(row, requests) == lax.rem(column, requests)) & (column <= row), 0.0, -1e30
    ).astype(F32)
    late_bias = jnp.concatenate(
        [jnp.concatenate([guest_bias] * steps, axis=0), fresh_bias], axis=1
    )

    loads[2].wait()
    query = jnp.concatenate(
        [
            query_v[t, :, g * head_dim : (g + 1) * head_dim].astype(F32)
            for g in range(portion)
            for t in range(steps)
        ],
        axis=0,
    ).astype(BF16)
    pl.semaphore_wait(barrier, greetings)
    loop(n_mp - 1, lambda k: leave_copy(k).start())
    loop(n_mp - 1, lambda k: page_copy(k).start())
    if n_inst > 2:
        for way in range(2):
            tell(way, 1)

    loads[1].wait()
    features = hidden_v[...].astype(F32).reshape(rows, hidden.shape[2]).astype(BF16)
    for j in range(kv_heads):
        weight_loads[j].wait()
        part_out[j] = dot(features, weight_v[j])
        if share == 1:
            if j < kv_heads - 1:
                part_copy(j, j).start()
        if j == 1 and n_inst > 2:
            hear(1)
    if share > 1:

        def send_part(k):
            to = lax.rem(mp + 1 + k, n_mp)
            j = lax.rem(to // share - own_head - 1 + 2 * kv_heads, kv_heads)
            part_copy(j, k).start()

        loop(n_mp - 1, send_part)

    scale = 1.0 / math.sqrt(head_dim)

    def with_ones(values):
        return jnp.concatenate([values, jnp.ones(values.shape, BF16)], axis=1)

    own_copies[1].wait()
    loop(n_mp - 1, lambda k: leave_copy(k).wait_recv())
    for far in range(2, n_inst - 1):
        hear(far)

    def take_moving(k):
        to = jnp.where(k < inst, k, k + 1)
        chosen = jnp.int32(0)
        for u in range(1, migrants):
            chosen = jnp.where(mig_dest[u, inst] == to, u, chosen)
        moving[k] = outgoing[chosen]
        move_copy(k).start()

    loop(n_inst - 1, take_moving)

    own_copies[0].wait()
    loop(n_mp - 1, lambda k: page_copy(k).wait_recv())
    held = cache[...].reshape(requests * context, pair)
    total_rows = portion * rows
    scores = dot(query, held[:, :head_dim], ((1,), (1,))) * scale
    scores = scores.reshape(portion * steps, requests, requests * context) + bias[None]
    scores = scores.reshape(total_rows, requests * context)
    peak = jnp.max(scores, axis=-1, keepdims=True)
    summed = weighted(jnp.exp(scores - peak), with_ones(held[:, head_dim:]))

    loads[3].wait()
    loop(n_mp - 1, lambda k: part_copy(0, k).wait_recv())
    projected = part_out[kv_heads - 1]
    for k in range(n_mp - 1):
        projected = projected + part_in[k]
    keys = projected[:, :head_dim]
    factor = lax.rsqrt(jnp.mean(keys * keys, axis=-1, keepdims=True) + 1e-06)
    keys = keys * factor * gain_v[...]
    keys = keys * cosine + pltpu.roll(keys, half, 1) * sine
    blank = jnp.zeros((128 - rows, head_dim), F32)
    fresh_keys = jnp.concatenate([keys, blank], axis=0).astype(BF16)
    fresh_values = jnp.concatenate([projected[:, head_dim:], blank], axis=0).astype(BF16)

    loop(n_inst - 1, move_wait)
    came = [arrived[place[v]].reshape(context, pair) for v in range(migrants)]
    late_keys = jnp.concatenate([page[:, :head_dim] for page in came] + [fresh_keys], axis=0)
    late_values = jnp.concatenate([page[:, head_dim:] for page in came] + [fresh_values], axis=0)
    late = dot(query, late_keys, ((1,), (1,))) * scale
    late = (late.reshape(portion, rows, guests + 128) + late_bias[None]).reshape(
        total_rows, guests + 128
    )
    highest = jnp.maximum(peak, jnp.max(late, axis=-1, keepdims=True))
    summed = summed * jnp.exp(peak - highest) + weighted(
        jnp.exp(late - highest), with_ones(late_values)
    )
    result = summed[:, :head_dim] / summed[:, head_dim:]
    for t in range(steps):
        for g in range(portion):
            at = (g * steps + t) * requests
            out[t, :, g * head_dim : (g + 1) * head_dim] = result[at : at + requests].astype(BF16)

    loop(n_mp - 1, lambda k: page_copy(k).wait_send())
    loop(n_mp - 1, lambda k: leave_copy(k).wait_send())
    loop(n_inst - 1, lambda k: move_copy(k).wait_send())
    loop(n_mp - 1, lambda k: part_copy(0, k).wait_send())


def local(
    n_inst,
    n_mp,
    hidden_states,
    kv_weight,
    key_gain,
    queries,
    kv_pool,
    page_table,
    lengths,
    mig_dest,
    mig_local,
    mig_slots,
):
    steps, requests, depth = hidden_states.shape
    head_dim = key_gain.shape[0]
    width = kv_weight.shape[1]
    pair = 2 * head_dim
    kv_heads = width // pair
    portion = queries.shape[2] // n_mp
    migrants = mig_dest.shape[1]
    pool = kv_pool[0]
    page = pool.shape[1]
    rows = steps * requests
    assert page_table.shape[1] == 1 and n_mp % kv_heads == 0
    far = pl.BlockSpec(memory_space=pltpu.HBM)
    return pl.pallas_call(
        functools.partial(kernel, n_inst, n_mp, migrants, kv_heads),
        out_shape=jax.ShapeDtypeStruct((steps, requests, portion), BF16),
        in_specs=[far] * 10,
        out_specs=pl.BlockSpec(memory_space=pltpu.VMEM),
        scratch_shapes=[
            pltpu.VMEM(pool.shape, BF16),
            pltpu.VMEM(hidden_states.shape, BF16),
            pltpu.VMEM((kv_heads, depth, pair), BF16),
            pltpu.VMEM((1, head_dim), F32),
            pltpu.VMEM((steps, requests, portion), BF16),
            pltpu.VMEM((requests, page, width), BF16),
            pltpu.VMEM((migrants, page, width), BF16),
            pltpu.VMEM((requests, n_mp, page, pair), BF16),
            pltpu.VMEM((migrants, n_mp, page, pair), BF16),
            pltpu.VMEM((n_inst - 1, n_mp, page, pair), BF16),
            pltpu.VMEM((n_inst - 1, n_mp, page, pair), BF16),
            pltpu.VMEM((kv_heads, rows, pair), F32),
            pltpu.VMEM((n_mp - 1, rows, pair), F32),
            pltpu.SMEM((requests,), jnp.int32),
            pltpu.SMEM((requests,), jnp.int32),
            pltpu.SMEM((migrants, n_inst), jnp.int32),
            pltpu.SMEM((migrants, n_inst), jnp.int32),
            pltpu.SMEM((migrants,), jnp.int32),
            pltpu.SemaphoreType.DMA((5,)),
            pltpu.SemaphoreType.DMA((4,)),
            pltpu.SemaphoreType.DMA((kv_heads,)),
            pltpu.SemaphoreType.DMA((2,)),
            pltpu.SemaphoreType.DMA((n_mp - 1,)),
            pltpu.SemaphoreType.DMA((n_mp - 1,)),
            pltpu.SemaphoreType.DMA((n_mp - 1,)),
            pltpu.SemaphoreType.DMA((n_mp - 1,)),
            pltpu.SemaphoreType.DMA((n_inst - 1,)),
            pltpu.SemaphoreType.DMA((n_inst - 1,)),
            pltpu.SemaphoreType.REGULAR((2, n_inst)),
            pltpu.SemaphoreType.DMA((n_mp - 1,)),
            pltpu.SemaphoreType.DMA((n_mp - 1,)),
        ],
        compiler_params=pltpu.CompilerParams(
            collective_id=0, has_side_effects=True, vmem_limit_bytes=32 * 1024 * 1024
        ),
    )(
        *[
            pltpu.with_memory_space_constraint(operand, pltpu.HBM)
            for operand in (
                page_table.reshape(-1),
                lengths,
                mig_dest.T,
                mig_local.T,
                mig_slots.reshape(-1),
                hidden_states,
                kv_weight,
                key_gain.reshape(1, head_dim),
                queries,
                pool,
            )
        ]
    )


def solution(mesh):
    placed = (
        P(None, ("groups", "inst"), "mp"),
        P("mp", None),
        P(),
        P(None, ("groups", "inst"), None),
        P(("groups", "inst"), "mp", None, None),
        P(("groups", "inst"), None, "mp"),
        P(("groups", "inst")),
        P("groups", None),
        P("groups", None),
        P(("groups", "inst"), None, None, "mp"),
    )
    return jax.shard_map(
        functools.partial(local, mesh.shape["inst"], mesh.shape["mp"]),
        mesh=mesh,
        in_specs=placed,
        out_specs=P(None, ("groups", "inst"), "mp"),
        check_vma=False,
    )
```

```python
import functools
import math

import jax
import jax.numpy as jnp
from jax import lax
from jax.experimental import pallas as pl
from jax.experimental.pallas import tpu as pltpu
from jax.sharding import PartitionSpec as P

MESH = pl.DeviceIdType.MESH
F32 = jnp.float32
BF16 = jnp.bfloat16


def loop(count, step):
    if count <= 4:
        for index in range(count):
            step(index)
    else:
        lax.fori_loop(0, count, lambda index, carry: (step(index), carry)[1], 0)


def dot(left, right, contract=((1,), (0,))):
    return lax.dot_general(left, right, (contract, ((), ())), preferred_element_type=F32)


def weighted(weights, values):
    high = weights.astype(BF16)
    low = (weights - high.astype(F32)).astype(BF16)
    return dot(high, values) + dot(low, values)


def kernel(
    n_inst,
    n_mp,
    migrants,
    kv_heads,
    table_h,
    length_h,
    dest_h,
    local_h,
    slot_h,
    hidden,
    weight,
    gain,
    queries,
    pool,
    out,
    pool_v,
    hidden_v,
    weight_v,
    gain_v,
    query_v,
    stage,
    leaving,
    cache,
    arrived,
    part_out,
    part_in,
    table,
    length,
    mig_dest,
    mig_local,
    mig_slot,
    int_sem,
    in_sem,
    weight_sem,
    own_sem,
    page_send,
    page_recv,
    move_send,
    move_recv,
    news,
    part_send,
    part_recv,
):
    inst = lax.axis_index("inst")
    mp = lax.axis_index("mp")
    steps, requests, _ = hidden.shape
    head_dim = gain.shape[1]
    pair = 2 * head_dim
    page = pool.shape[1]
    rows = steps * requests
    portion = query_v.shape[2] // head_dim
    share = n_mp // kv_heads
    context = n_mp * page
    own_head = mp // share

    def columns(head):
        return pl.ds(pl.multiple_of(head * pair, pair), pair)

    barrier = pltpu.get_barrier_semaphore()

    def greet_peer(k):
        pl.semaphore_signal(
            barrier,
            inc=1,
            device_id={"inst": inst, "mp": lax.rem(mp + 1 + k, n_mp)},
            device_id_type=MESH,
        )

    loop(n_mp - 1, greet_peer)
    for away, there in ((1, inst < n_inst - 1), (-1, inst > 0)):

        @pl.when(there)
        def _():
            pl.semaphore_signal(
                barrier, inc=1, device_id={"inst": inst + away, "mp": mp}, device_id_type=MESH
            )

    greetings = (
        n_mp - 1 + jnp.where(inst < n_inst - 1, 1, 0) + jnp.where(inst > 0, 1, 0)
    )

    loads = [
        pltpu.make_async_copy(pool, pool_v, in_sem.at[0]),
        pltpu.make_async_copy(hidden, hidden_v, in_sem.at[1]),
        pltpu.make_async_copy(
            queries.at[
                :,
                :,
                pl.ds(pl.multiple_of(mp * (portion * head_dim), head_dim), portion * head_dim),
            ],
            query_v,
            in_sem.at[2],
        ),
        pltpu.make_async_copy(gain, gain_v, in_sem.at[3]),
    ]
    heads = [lax.rem(own_head + 1 + j, kv_heads) for j in range(kv_heads)]
    weight_loads = [
        pltpu.make_async_copy(weight.at[:, columns(head)], weight_v.at[j], weight_sem.at[j])
        for j, head in enumerate(heads)
    ]
    int_loads = [
        pltpu.make_async_copy(source, target, int_sem.at[n])
        for n, (source, target) in enumerate(
            [
                (table_h, table),
                (slot_h, mig_slot),
                (dest_h, mig_dest),
                (local_h, mig_local),
                (length_h, length),
            ]
        )
    ]
    loads[0].start()
    for load in int_loads:
        load.start()
    loads[1].start()
    loads[2].start()
    loads[3].start()
    for load in weight_loads:
        load.start()

    for load in int_loads:
        load.wait()
    loads[0].wait()
    for r in range(requests):
        stage[r] = pool_v[table[r]]

    def take_leaving(k):
        to_inst = jnp.where(k < inst, k, k + 1)
        slot = mig_slot[0]
        for u in range(1, migrants):
            slot = jnp.where(mig_dest[u, inst] == to_inst, mig_slot[u], slot)
        leaving[k] = pool_v[slot]

    loop(n_inst - 1, take_leaving)

    def page_copy(k):
        to = lax.rem(mp + 1 + k, n_mp)
        return pltpu.make_async_remote_copy(
            src_ref=stage.at[:, :, columns(to // share)],
            dst_ref=cache.at[pl.ds(0, requests), mp],
            send_sem=page_send.at[k],
            recv_sem=page_recv.at[k],
            device_id={"inst": inst, "mp": to},
            device_id_type=MESH,
        )

    def move_copy(way, far, to):
        target = inst + (1 + far) * (1 - 2 * way)
        place = target - 1 + way
        here = inst - way
        return pltpu.make_async_remote_copy(
            src_ref=leaving.at[place, :, columns(to // share)],
            dst_ref=arrived.at[here, mp],
            send_sem=move_send.at[place, to],
            recv_sem=move_recv.at[here, mp],
            device_id={"inst": target, "mp": to},
            device_id_type=MESH,
        )

    def move_wait(k, column):
        pltpu.make_async_remote_copy(
            src_ref=leaving.at[k, :, columns(0)],
            dst_ref=arrived.at[k, column],
            send_sem=move_send.at[k, column],
            recv_sem=move_recv.at[k, column],
            device_id={"inst": jnp.where(k < inst, k, k + 1), "mp": column},
            device_id_type=MESH,
        ).wait_recv()

    def line(way):
        return inst if way == 0 else n_inst - 1 - inst

    def tell(way, far):
        @pl.when((line(way) > 0) & (line(way) + far <= n_inst - 1))
        def _():
            pl.semaphore_signal(
                news.at[way, far],
                inc=1,
                device_id={"inst": inst - 1 + 2 * way, "mp": mp},
                device_id_type=MESH,
            )

    def hear(far):
        for way in range(2):

            @pl.when(line(way) + 1 + far <= n_inst - 1)
            def _():
                pl.semaphore_wait(news.at[way, far], 1)

            if far + 1 <= n_inst - 2:
                tell(way, far + 1)

            @pl.when(line(way) + 1 + far <= n_inst - 1)
            def _():
                loop(n_mp, lambda to: move_copy(way, far, to).start())

    def part_copy(j, k):
        to = lax.rem(mp + 1 + k, n_mp)
        return pltpu.make_async_remote_copy(
            src_ref=part_out.at[j],
            dst_ref=part_in.at[k],
            send_sem=part_send.at[k],
            recv_sem=part_recv.at[k],
            device_id={"inst": inst, "mp": to},
            device_id_type=MESH,
        )

    own_copies = [
        pltpu.make_async_copy(
            stage.at[:, :, columns(own_head)], cache.at[pl.ds(0, requests), mp], own_sem.at[0]
        ),
    ]
    for copy in own_copies:
        copy.start()

    count = jnp.int32(0)
    place = [jnp.int32(0)] * migrants
    guest = [jnp.int32(-1)] * migrants
    for k in range(n_inst - 1):
        source = jnp.where(k < inst, k, k + 1)
        for u in range(migrants):
            here = mig_dest[u, source] == inst
            for v in range(migrants):
                hit = here & (count == v)
                place[v] = jnp.where(hit, k, place[v])
                guest[v] = jnp.where(hit, mig_local[u, source], guest[v])
            count = count + jnp.where(here, 1, 0)

    row8 = lax.broadcasted_iota(jnp.int32, (requests, head_dim), 0)
    length8 = jnp.zeros((requests, head_dim), jnp.int32)
    for r in range(requests):
        length8 = jnp.where(row8 == r, length[r], length8)

    half = head_dim // 2
    lane = lax.broadcasted_iota(jnp.int32, (rows, head_dim), 1)
    pair_index = jnp.where(lane < half, lane, lane - half)
    frequency = jnp.exp(-(2.0 * pair_index.astype(F32) / head_dim) * math.log(1000000.0))
    position = jnp.concatenate([(length8 + t).astype(F32) for t in range(steps)], axis=0)
    angle = position * frequency
    cosine = jnp.cos(angle)
    sine = jnp.sin(angle)
    sine = jnp.where(lane < half, -sine, sine)

    stay8 = length8
    for v in range(migrants):
        stay8 = jnp.where(row8 == guest[v], 0, stay8)
    cached_lane = lax.broadcasted_iota(jnp.int32, (requests, requests * context), 1)
    first = lax.broadcasted_iota(jnp.int32, (requests, requests * context), 0) * context
    last = first + jnp.broadcast_to(stay8[:, :1], first.shape)
    bias = jnp.where((cached_lane >= first) & (cached_lane < last), 0.0, -1e30).astype(F32)

    guests = migrants * context
    guest_lane = lax.broadcasted_iota(jnp.int32, (requests, guests), 1)
    guest_row = lax.broadcasted_iota(jnp.int32, (requests, guests), 0)
    guest_length = jnp.broadcast_to(length8[:, :1], guest_lane.shape)
    known = guest_row < 0
    for v in range(migrants):
        known = known | (
            (guest_row == guest[v])
            & (guest_lane >= v * context)
            & (guest_lane < v * context + guest_length)
        )
    guest_bias = jnp.where(known, 0.0, -1e30).astype(F32)
    row = lax.broadcasted_iota(jnp.int32, (rows, 128), 0)
    column = lax.broadcasted_iota(jnp.int32, (rows, 128), 1)
    fresh_bias = jnp.where(
        (lax.rem(row, requests) == lax.rem(column, requests)) & (column <= row), 0.0, -1e30
    ).astype(F32)
    late_bias = jnp.concatenate(
        [jnp.concatenate([guest_bias] * steps, axis=0), fresh_bias], axis=1
    )

    loads[2].wait()
    query = jnp.concatenate(
        [
            query_v[t, :, g * head_dim : (g + 1) * head_dim].astype(F32)
            for g in range(portion)
            for t in range(steps)
        ],
        axis=0,
    ).astype(BF16)
    pl.semaphore_wait(barrier, greetings)
    loop(n_mp - 1, lambda k: page_copy(k).start())
    for way in range(2):
        tell(way, 0)

    loads[1].wait()
    features = hidden_v[...].astype(F32).reshape(rows, hidden.shape[2]).astype(BF16)
    for j in range(kv_heads):
        weight_loads[j].wait()
        part_out[j] = dot(features, weight_v[j])
        if share == 1:
            if j < kv_heads - 1:
                part_copy(j, j).start()
        if j % 2 == 1 and j // 2 < n_inst - 1:
            hear(j // 2)
    if share > 1:

        def send_part(k):
            to = lax.rem(mp + 1 + k, n_mp)
            j = lax.rem(to // share - own_head - 1 + 2 * kv_heads, kv_heads)
            part_copy(j, k).start()

        loop(n_mp - 1, send_part)

    scale = 1.0 / math.sqrt(head_dim)

    def with_ones(values):
        return jnp.concatenate([values, jnp.ones(values.shape, BF16)], axis=1)

    for far in range(min(kv_heads // 2, n_inst - 1), n_inst - 1):
        hear(far)

    own_copies[0].wait()
    loop(n_mp - 1, lambda k: page_copy(k).wait_recv())
    held = cache[...].reshape(requests * context, pair)
    total_rows = portion * rows
    scores = dot(query, held[:, :head_dim], ((1,), (1,))) * scale
    scores = scores.reshape(portion * steps, requests, requests * context) + bias[None]
    scores = scores.reshape(total_rows, requests * context)
    peak = jnp.max(scores, axis=-1, keepdims=True)
    summed = weighted(jnp.exp(scores - peak), with_ones(held[:, head_dim:]))

    loads[3].wait()
    loop(n_mp - 1, lambda k: part_copy(0, k).wait_recv())
    projected = part_out[kv_heads - 1]
    for k in range(n_mp - 1):
        projected = projected + part_in[k]
    keys = projected[:, :head_dim]
    factor = lax.rsqrt(jnp.mean(keys * keys, axis=-1, keepdims=True) + 1e-06)
    keys = keys * factor * gain_v[...]
    keys = keys * cosine + pltpu.roll(keys, half, 1) * sine
    blank = jnp.zeros((128 - rows, head_dim), F32)
    fresh_keys = jnp.concatenate([keys, blank], axis=0).astype(BF16)
    fresh_values = jnp.concatenate([projected[:, head_dim:], blank], axis=0).astype(BF16)

    loop(n_inst - 1, lambda k: loop(n_mp, lambda column: move_wait(k, column)))
    came = [arrived[place[v]].reshape(context, pair) for v in range(migrants)]
    late_keys = jnp.concatenate([page[:, :head_dim] for page in came] + [fresh_keys], axis=0)
    late_values = jnp.concatenate([page[:, head_dim:] for page in came] + [fresh_values], axis=0)
    late = dot(query, late_keys, ((1,), (1,))) * scale
    late = (late.reshape(portion, rows, guests + 128) + late_bias[None]).reshape(
        total_rows, guests + 128
    )
    highest = jnp.maximum(peak, jnp.max(late, axis=-1, keepdims=True))
    summed = summed * jnp.exp(peak - highest) + weighted(
        jnp.exp(late - highest), with_ones(late_values)
    )
    result = summed[:, :head_dim] / summed[:, head_dim:]
    for t in range(steps):
        for g in range(portion):
            at = (g * steps + t) * requests
            out[t, :, g * head_dim : (g + 1) * head_dim] = result[at : at + requests].astype(BF16)

    loop(n_mp - 1, lambda k: page_copy(k).wait_send())
    for far in range(n_inst - 1):
        for way in range(2):

            @pl.when(line(way) + 1 + far <= n_inst - 1)
            def _():
                loop(n_mp, lambda to: move_copy(way, far, to).wait_send())

    loop(n_mp - 1, lambda k: part_copy(0, k).wait_send())


def local(
    n_inst,
    n_mp,
    hidden_states,
    kv_weight,
    key_gain,
    queries,
    kv_pool,
    page_table,
    lengths,
    mig_dest,
    mig_local,
    mig_slots,
):
    steps, requests, depth = hidden_states.shape
    head_dim = key_gain.shape[0]
    width = kv_weight.shape[1]
    pair = 2 * head_dim
    kv_heads = width // pair
    portion = queries.shape[2] // n_mp
    migrants = mig_dest.shape[1]
    pool = kv_pool[0]
    page = pool.shape[1]
    rows = steps * requests
    assert page_table.shape[1] == 1 and n_mp % kv_heads == 0
    far = pl.BlockSpec(memory_space=pltpu.HBM)
    return pl.pallas_call(
        functools.partial(kernel, n_inst, n_mp, migrants, kv_heads),
        out_shape=jax.ShapeDtypeStruct((steps, requests, portion), BF16),
        in_specs=[far] * 10,
        out_specs=pl.BlockSpec(memory_space=pltpu.VMEM),
        scratch_shapes=[
            pltpu.VMEM(pool.shape, BF16),
            pltpu.VMEM(hidden_states.shape, BF16),
            pltpu.VMEM((kv_heads, depth, pair), BF16),
            pltpu.VMEM((1, head_dim), F32),
            pltpu.VMEM((steps, requests, portion), BF16),
            pltpu.VMEM((requests, page, width), BF16),
            pltpu.VMEM((n_inst - 1, page, width), BF16),
            pltpu.VMEM((requests, n_mp, page, pair), BF16),
            pltpu.VMEM((n_inst - 1, n_mp, page, pair), BF16),
            pltpu.VMEM((kv_heads, rows, pair), F32),
            pltpu.VMEM((n_mp - 1, rows, pair), F32),
            pltpu.SMEM((requests,), jnp.int32),
            pltpu.SMEM((requests,), jnp.int32),
            pltpu.SMEM((migrants, n_inst), jnp.int32),
            pltpu.SMEM((migrants, n_inst), jnp.int32),
            pltpu.SMEM((migrants,), jnp.int32),
            pltpu.SemaphoreType.DMA((5,)),
            pltpu.SemaphoreType.DMA((4,)),
            pltpu.SemaphoreType.DMA((kv_heads,)),
            pltpu.SemaphoreType.DMA((2,)),
            pltpu.SemaphoreType.DMA((n_mp - 1,)),
            pltpu.SemaphoreType.DMA((n_mp - 1,)),
            pltpu.SemaphoreType.DMA((n_inst - 1, n_mp)),
            pltpu.SemaphoreType.DMA((n_inst - 1, n_mp)),
            pltpu.SemaphoreType.REGULAR((2, n_inst)),
            pltpu.SemaphoreType.DMA((n_mp - 1,)),
            pltpu.SemaphoreType.DMA((n_mp - 1,)),
        ],
        compiler_params=pltpu.CompilerParams(
            collective_id=0, has_side_effects=True, vmem_limit_bytes=32 * 1024 * 1024
        ),
    )(
        *[
            pltpu.with_memory_space_constraint(operand, pltpu.HBM)
            for operand in (
                page_table.reshape(-1),
                lengths,
                mig_dest.T,
                mig_local.T,
                mig_slots.reshape(-1),
                hidden_states,
                kv_weight,
                key_gain.reshape(1, head_dim),
                queries,
                pool,
            )
        ]
    )


def solution(mesh):
    placed = (
        P(None, ("groups", "inst"), "mp"),
        P("mp", None),
        P(),
        P(None, ("groups", "inst"), None),
        P(("groups", "inst"), "mp", None, None),
        P(("groups", "inst"), None, "mp"),
        P(("groups", "inst")),
        P("groups", None),
        P("groups", None),
        P(("groups", "inst"), None, None, "mp"),
    )
    return jax.shard_map(
        functools.partial(local, mesh.shape["inst"], mesh.shape["mp"]),
        mesh=mesh,
        in_specs=placed,
        out_specs=P(None, ("groups", "inst"), "mp"),
        check_vma=False,
    )
```

```python
import functools
import math

import jax
import jax.numpy as jnp
from jax import lax
from jax.experimental import pallas as pl
from jax.experimental.pallas import tpu as pltpu
from jax.sharding import PartitionSpec as P

MESH = pl.DeviceIdType.MESH
F32 = jnp.float32
BF16 = jnp.bfloat16


def loop(count, step):
    if count <= 4:
        for index in range(count):
            step(index)
    else:
        lax.fori_loop(0, count, lambda index, carry: (step(index), carry)[1], 0)


def dot(left, right, contract=((1,), (0,))):
    return lax.dot_general(left, right, (contract, ((), ())), preferred_element_type=F32)


def weighted(weights, values):
    high = weights.astype(BF16)
    low = (weights - high.astype(F32)).astype(BF16)
    return dot(high, values) + dot(low, values)


def kernel(
    n_inst,
    n_mp,
    migrants,
    kv_heads,
    table_h,
    length_h,
    dest_h,
    local_h,
    slot_h,
    hidden,
    weight,
    gain,
    queries,
    pool,
    out,
    pool_v,
    hidden_v,
    weight_v,
    gain_v,
    query_v,
    stage,
    leaving,
    cache,
    arrived,
    part_out,
    part_in,
    table,
    length,
    mig_dest,
    mig_local,
    mig_slot,
    int_sem,
    in_sem,
    weight_sem,
    own_sem,
    page_send,
    page_recv,
    move_send,
    move_recv,
    news,
    part_send,
    part_recv,
):
    inst = lax.axis_index("inst")
    mp = lax.axis_index("mp")
    steps, requests, _ = hidden.shape
    head_dim = gain.shape[1]
    pair = 2 * head_dim
    page = pool.shape[1]
    rows = steps * requests
    portion = query_v.shape[2] // head_dim
    share = n_mp // kv_heads
    context = n_mp * page
    own_head = mp // share

    def columns(head):
        return pl.ds(pl.multiple_of(head * pair, pair), pair)

    barrier = pltpu.get_barrier_semaphore()

    def greet_peer(k):
        pl.semaphore_signal(
            barrier,
            inc=1,
            device_id={"inst": inst, "mp": lax.rem(mp + 1 + k, n_mp)},
            device_id_type=MESH,
        )

    loop(n_mp - 1, greet_peer)
    for away, there in ((1, inst < n_inst - 1), (-1, inst > 0)):

        @pl.when(there)
        def _():
            pl.semaphore_signal(
                barrier, inc=1, device_id={"inst": inst + away, "mp": mp}, device_id_type=MESH
            )

    greetings = (
        n_mp - 1 + jnp.where(inst < n_inst - 1, 1, 0) + jnp.where(inst > 0, 1, 0)
    )

    loads = [
        pltpu.make_async_copy(pool, pool_v, in_sem.at[0]),
        pltpu.make_async_copy(hidden, hidden_v, in_sem.at[1]),
        pltpu.make_async_copy(
            queries.at[
                :,
                :,
                pl.ds(pl.multiple_of(mp * (portion * head_dim), head_dim), portion * head_dim),
            ],
            query_v,
            in_sem.at[2],
        ),
        pltpu.make_async_copy(gain, gain_v, in_sem.at[3]),
    ]
    heads = [lax.rem(own_head + 1 + j, kv_heads) for j in range(kv_heads)]
    weight_loads = [
        pltpu.make_async_copy(weight.at[:, columns(head)], weight_v.at[j], weight_sem.at[j])
        for j, head in enumerate(heads)
    ]
    int_loads = [
        pltpu.make_async_copy(source, target, int_sem.at[n])
        for n, (source, target) in enumerate(
            [
                (table_h, table),
                (slot_h, mig_slot),
                (dest_h, mig_dest),
                (local_h, mig_local),
                (length_h, length),
            ]
        )
    ]
    loads[0].start()
    for load in int_loads:
        load.start()
    loads[1].start()
    loads[2].start()
    loads[3].start()
    for load in weight_loads:
        load.start()

    for load in int_loads:
        load.wait()
    loads[0].wait()
    for r in range(requests):
        stage[r] = pool_v[table[r]]

    def take_leaving(k):
        to_inst = jnp.where(k < inst, k, k + 1)
        slot = mig_slot[0]
        for u in range(1, migrants):
            slot = jnp.where(mig_dest[u, inst] == to_inst, mig_slot[u], slot)
        leaving[k] = pool_v[slot]

    loop(n_inst - 1, take_leaving)

    def page_copy(k):
        to = lax.rem(mp + 1 + k, n_mp)
        return pltpu.make_async_remote_copy(
            src_ref=stage.at[:, :, columns(to // share)],
            dst_ref=cache.at[pl.ds(0, requests), mp],
            send_sem=page_send.at[k],
            recv_sem=page_recv.at[k],
            device_id={"inst": inst, "mp": to},
            device_id_type=MESH,
        )

    def move_copy(way, far, to):
        target = inst + (1 + far) * (1 - 2 * way)
        place = target - 1 + way
        here = inst - way
        return pltpu.make_async_remote_copy(
            src_ref=leaving.at[place, :, columns(to // share)],
            dst_ref=arrived.at[here, mp],
            send_sem=move_send.at[place, to],
            recv_sem=move_recv.at[here, mp],
            device_id={"inst": target, "mp": to},
            device_id_type=MESH,
        )

    def move_wait(k, column):
        pltpu.make_async_remote_copy(
            src_ref=leaving.at[k, :, columns(0)],
            dst_ref=arrived.at[k, column],
            send_sem=move_send.at[k, column],
            recv_sem=move_recv.at[k, column],
            device_id={"inst": jnp.where(k < inst, k, k + 1), "mp": column},
            device_id_type=MESH,
        ).wait_recv()

    def line(way):
        return inst if way == 0 else n_inst - 1 - inst

    def tell(way, far):
        @pl.when((line(way) > 0) & (line(way) + far <= n_inst - 1))
        def _():
            pl.semaphore_signal(
                news.at[way, far],
                inc=1,
                device_id={"inst": inst - 1 + 2 * way, "mp": mp},
                device_id_type=MESH,
            )

    def hear(far):
        for way in range(2):

            @pl.when(line(way) + 1 + far <= n_inst - 1)
            def _():
                pl.semaphore_wait(news.at[way, far], 1)

            if far + 1 <= n_inst - 2:
                tell(way, far + 1)

            @pl.when(line(way) + 1 + far <= n_inst - 1)
            def _():
                loop(n_mp, lambda to: move_copy(way, far, to).start())

    def part_copy(j, k):
        to = lax.rem(mp + 1 + k, n_mp)
        return pltpu.make_async_remote_copy(
            src_ref=part_out.at[j],
            dst_ref=part_in.at[k],
            send_sem=part_send.at[k],
            recv_sem=part_recv.at[k],
            device_id={"inst": inst, "mp": to},
            device_id_type=MESH,
        )

    own_copies = [
        pltpu.make_async_copy(
            stage.at[:, :, columns(own_head)], cache.at[pl.ds(0, requests), mp], own_sem.at[0]
        ),
    ]
    for copy in own_copies:
        copy.start()

    count = jnp.int32(0)
    place = [jnp.int32(0)] * migrants
    guest = [jnp.int32(-1)] * migrants
    for k in range(n_inst - 1):
        source = jnp.where(k < inst, k, k + 1)
        for u in range(migrants):
            here = mig_dest[u, source] == inst
            for v in range(migrants):
                hit = here & (count == v)
                place[v] = jnp.where(hit, k, place[v])
                guest[v] = jnp.where(hit, mig_local[u, source], guest[v])
            count = count + jnp.where(here, 1, 0)

    row8 = lax.broadcasted_iota(jnp.int32, (requests, head_dim), 0)
    length8 = jnp.zeros((requests, head_dim), jnp.int32)
    for r in range(requests):
        length8 = jnp.where(row8 == r, length[r], length8)

    half = head_dim // 2
    lane = lax.broadcasted_iota(jnp.int32, (rows, head_dim), 1)
    pair_index = jnp.where(lane < half, lane, lane - half)
    frequency = jnp.exp(-(2.0 * pair_index.astype(F32) / head_dim) * math.log(1000000.0))
    position = jnp.concatenate([(length8 + t).astype(F32) for t in range(steps)], axis=0)
    angle = position * frequency
    cosine = jnp.cos(angle)
    sine = jnp.sin(angle)
    sine = jnp.where(lane < half, -sine, sine)

    stay8 = length8
    for v in range(migrants):
        stay8 = jnp.where(row8 == guest[v], 0, stay8)
    cached_lane = lax.broadcasted_iota(jnp.int32, (requests, requests * context), 1)
    first = lax.broadcasted_iota(jnp.int32, (requests, requests * context), 0) * context
    last = first + jnp.broadcast_to(stay8[:, :1], first.shape)
    bias = jnp.where((cached_lane >= first) & (cached_lane < last), 0.0, -1e30).astype(F32)

    guests = migrants * context
    guest_lane = lax.broadcasted_iota(jnp.int32, (requests, guests), 1)
    guest_row = lax.broadcasted_iota(jnp.int32, (requests, guests), 0)
    guest_length = jnp.broadcast_to(length8[:, :1], guest_lane.shape)
    known = guest_row < 0
    for v in range(migrants):
        known = known | (
            (guest_row == guest[v])
            & (guest_lane >= v * context)
            & (guest_lane < v * context + guest_length)
        )
    guest_bias = jnp.where(known, 0.0, -1e30).astype(F32)
    row = lax.broadcasted_iota(jnp.int32, (rows, 128), 0)
    column = lax.broadcasted_iota(jnp.int32, (rows, 128), 1)
    fresh_bias = jnp.where(
        (lax.rem(row, requests) == lax.rem(column, requests)) & (column <= row), 0.0, -1e30
    ).astype(F32)
    loads[2].wait()
    query = jnp.concatenate(
        [
            query_v[t, :, g * head_dim : (g + 1) * head_dim].astype(F32)
            for g in range(portion)
            for t in range(steps)
        ],
        axis=0,
    ).astype(BF16)
    pl.semaphore_wait(barrier, greetings)
    loop(n_mp - 1, lambda k: page_copy(k).start())
    for way in range(2):
        tell(way, 0)

    loads[1].wait()
    features = hidden_v[...].astype(F32).reshape(rows, hidden.shape[2]).astype(BF16)
    for j in range(kv_heads):
        weight_loads[j].wait()
        part_out[j] = dot(features, weight_v[j])
        if share == 1:
            if j < kv_heads - 1:
                part_copy(j, j).start()
        if j < n_inst - 1:
            hear(j)
    if share > 1:

        def send_part(k):
            to = lax.rem(mp + 1 + k, n_mp)
            j = lax.rem(to // share - own_head - 1 + 2 * kv_heads, kv_heads)
            part_copy(j, k).start()

        loop(n_mp - 1, send_part)

    scale = 1.0 / math.sqrt(head_dim)

    def with_ones(values):
        return jnp.concatenate([values, jnp.ones(values.shape, BF16)], axis=1)

    for far in range(min(kv_heads, n_inst - 1), n_inst - 1):
        hear(far)

    own_copies[0].wait()
    loop(n_mp - 1, lambda k: page_copy(k).wait_recv())
    held = cache[...].reshape(requests * context, pair)
    total_rows = portion * rows
    scores = dot(query, held[:, :head_dim], ((1,), (1,))) * scale
    scores = scores.reshape(portion * steps, requests, requests * context) + bias[None]
    scores = scores.reshape(total_rows, requests * context)
    peak = jnp.max(scores, axis=-1, keepdims=True)
    summed = weighted(jnp.exp(scores - peak), with_ones(held[:, head_dim:]))

    loads[3].wait()
    loop(n_mp - 1, lambda k: part_copy(0, k).wait_recv())
    projected = part_out[kv_heads - 1]
    for k in range(n_mp - 1):
        projected = projected + part_in[k]
    keys = projected[:, :head_dim]
    factor = lax.rsqrt(jnp.mean(keys * keys, axis=-1, keepdims=True) + 1e-06)
    keys = keys * factor * gain_v[...]
    keys = keys * cosine + pltpu.roll(keys, half, 1) * sine
    blank = jnp.zeros((128 - rows, head_dim), F32)
    fresh_keys = jnp.concatenate([keys, blank], axis=0).astype(BF16)
    fresh_values = jnp.concatenate([projected[:, head_dim:], blank], axis=0).astype(BF16)

    fresh = dot(query, fresh_keys, ((1,), (1,))) * scale
    fresh = (fresh.reshape(portion, rows, 128) + fresh_bias[None]).reshape(total_rows, 128)
    highest = jnp.maximum(peak, jnp.max(fresh, axis=-1, keepdims=True))
    summed = summed * jnp.exp(peak - highest) + weighted(
        jnp.exp(fresh - highest), with_ones(fresh_values)
    )

    loop(n_inst - 1, lambda k: loop(n_mp, lambda column: move_wait(k, column)))
    came = jnp.concatenate(
        [arrived[place[v]].reshape(context, pair) for v in range(migrants)], axis=0
    )
    late = dot(query, came[:, :head_dim], ((1,), (1,))) * scale
    late = late.reshape(portion * steps, requests, guests) + guest_bias[None]
    late = late.reshape(total_rows, guests)
    peak = highest
    highest = jnp.maximum(peak, jnp.max(late, axis=-1, keepdims=True))
    summed = summed * jnp.exp(peak - highest) + weighted(
        jnp.exp(late - highest), with_ones(came[:, head_dim:])
    )
    result = summed[:, :head_dim] / summed[:, head_dim:]
    for t in range(steps):
        for g in range(portion):
            at = (g * steps + t) * requests
            out[t, :, g * head_dim : (g + 1) * head_dim] = result[at : at + requests].astype(BF16)

    loop(n_mp - 1, lambda k: page_copy(k).wait_send())
    for far in range(n_inst - 1):
        for way in range(2):

            @pl.when(line(way) + 1 + far <= n_inst - 1)
            def _():
                loop(n_mp, lambda to: move_copy(way, far, to).wait_send())

    loop(n_mp - 1, lambda k: part_copy(0, k).wait_send())


def local(
    n_inst,
    n_mp,
    hidden_states,
    kv_weight,
    key_gain,
    queries,
    kv_pool,
    page_table,
    lengths,
    mig_dest,
    mig_local,
    mig_slots,
):
    steps, requests, depth = hidden_states.shape
    head_dim = key_gain.shape[0]
    width = kv_weight.shape[1]
    pair = 2 * head_dim
    kv_heads = width // pair
    portion = queries.shape[2] // n_mp
    migrants = mig_dest.shape[1]
    pool = kv_pool[0]
    page = pool.shape[1]
    rows = steps * requests
    assert page_table.shape[1] == 1 and n_mp % kv_heads == 0
    far = pl.BlockSpec(memory_space=pltpu.HBM)
    return pl.pallas_call(
        functools.partial(kernel, n_inst, n_mp, migrants, kv_heads),
        out_shape=jax.ShapeDtypeStruct((steps, requests, portion), BF16),
        in_specs=[far] * 10,
        out_specs=pl.BlockSpec(memory_space=pltpu.VMEM),
        scratch_shapes=[
            pltpu.VMEM(pool.shape, BF16),
            pltpu.VMEM(hidden_states.shape, BF16),
            pltpu.VMEM((kv_heads, depth, pair), BF16),
            pltpu.VMEM((1, head_dim), F32),
            pltpu.VMEM((steps, requests, portion), BF16),
            pltpu.VMEM((requests, page, width), BF16),
            pltpu.VMEM((n_inst - 1, page, width), BF16),
            pltpu.VMEM((requests, n_mp, page, pair), BF16),
            pltpu.VMEM((n_inst - 1, n_mp, page, pair), BF16),
            pltpu.VMEM((kv_heads, rows, pair), F32),
            pltpu.VMEM((n_mp - 1, rows, pair), F32),
            pltpu.SMEM((requests,), jnp.int32),
            pltpu.SMEM((requests,), jnp.int32),
            pltpu.SMEM((migrants, n_inst), jnp.int32),
            pltpu.SMEM((migrants, n_inst), jnp.int32),
            pltpu.SMEM((migrants,), jnp.int32),
            pltpu.SemaphoreType.DMA((5,)),
            pltpu.SemaphoreType.DMA((4,)),
            pltpu.SemaphoreType.DMA((kv_heads,)),
            pltpu.SemaphoreType.DMA((2,)),
            pltpu.SemaphoreType.DMA((n_mp - 1,)),
            pltpu.SemaphoreType.DMA((n_mp - 1,)),
            pltpu.SemaphoreType.DMA((n_inst - 1, n_mp)),
            pltpu.SemaphoreType.DMA((n_inst - 1, n_mp)),
            pltpu.SemaphoreType.REGULAR((2, n_inst)),
            pltpu.SemaphoreType.DMA((n_mp - 1,)),
            pltpu.SemaphoreType.DMA((n_mp - 1,)),
        ],
        compiler_params=pltpu.CompilerParams(
            collective_id=0, has_side_effects=True, vmem_limit_bytes=32 * 1024 * 1024
        ),
    )(
        *[
            pltpu.with_memory_space_constraint(operand, pltpu.HBM)
            for operand in (
                page_table.reshape(-1),
                lengths,
                mig_dest.T,
                mig_local.T,
                mig_slots.reshape(-1),
                hidden_states,
                kv_weight,
                key_gain.reshape(1, head_dim),
                queries,
                pool,
            )
        ]
    )


def solution(mesh):
    placed = (
        P(None, ("groups", "inst"), "mp"),
        P("mp", None),
        P(),
        P(None, ("groups", "inst"), None),
        P(("groups", "inst"), "mp", None, None),
        P(("groups", "inst"), None, "mp"),
        P(("groups", "inst")),
        P("groups", None),
        P("groups", None),
        P(("groups", "inst"), None, None, "mp"),
    )
    return jax.shard_map(
        functools.partial(local, mesh.shape["inst"], mesh.shape["mp"]),
        mesh=mesh,
        in_specs=placed,
        out_specs=P(None, ("groups", "inst"), "mp"),
        check_vma=False,
    )
```

```python
import functools
import math

import jax
import jax.numpy as jnp
from jax import lax
from jax.experimental import pallas as pl
from jax.experimental.pallas import tpu as pltpu
from jax.sharding import PartitionSpec as P

MESH = pl.DeviceIdType.MESH
F32 = jnp.float32
BF16 = jnp.bfloat16


def loop(count, step):
    if count <= 4:
        for index in range(count):
            step(index)
    else:
        lax.fori_loop(0, count, lambda index, carry: (step(index), carry)[1], 0)


def dot(left, right, contract=((1,), (0,))):
    return lax.dot_general(left, right, (contract, ((), ())), preferred_element_type=F32)


def weighted(weights, values):
    high = weights.astype(BF16)
    low = (weights - high.astype(F32)).astype(BF16)
    return dot(high, values) + dot(low, values)


def kernel(
    n_inst,
    n_mp,
    migrants,
    kv_heads,
    table_h,
    length_h,
    dest_h,
    local_h,
    slot_h,
    hidden,
    weight,
    gain,
    queries,
    pool,
    out,
    pool_v,
    hidden_v,
    weight_v,
    gain_v,
    query_v,
    stage,
    leaving,
    cache,
    arrived,
    part_out,
    part_in,
    table,
    length,
    mig_dest,
    mig_local,
    mig_slot,
    int_sem,
    in_sem,
    weight_sem,
    own_sem,
    page_send,
    page_recv,
    move_send,
    move_recv,
    news,
    part_send,
    part_recv,
):
    inst = lax.axis_index("inst")
    mp = lax.axis_index("mp")
    steps, requests, _ = hidden.shape
    head_dim = gain.shape[1]
    pair = 2 * head_dim
    page = pool.shape[1]
    rows = steps * requests
    portion = query_v.shape[2] // head_dim
    share = n_mp // kv_heads
    context = n_mp * page
    own_head = mp // share

    def columns(head):
        return pl.ds(pl.multiple_of(head * pair, pair), pair)

    barrier = pltpu.get_barrier_semaphore()

    def greet_peer(k):
        pl.semaphore_signal(
            barrier,
            inc=1,
            device_id={"inst": inst, "mp": lax.rem(mp + 1 + k, n_mp)},
            device_id_type=MESH,
        )

    loop(n_mp - 1, greet_peer)
    for away, there in ((1, inst < n_inst - 1), (-1, inst > 0)):

        @pl.when(there)
        def _():
            pl.semaphore_signal(
                barrier, inc=1, device_id={"inst": inst + away, "mp": mp}, device_id_type=MESH
            )

    greetings = (
        n_mp - 1 + jnp.where(inst < n_inst - 1, 1, 0) + jnp.where(inst > 0, 1, 0)
    )

    loads = [
        pltpu.make_async_copy(pool, pool_v, in_sem.at[0]),
        pltpu.make_async_copy(hidden, hidden_v, in_sem.at[1]),
        pltpu.make_async_copy(
            queries.at[
                :,
                :,
                pl.ds(pl.multiple_of(mp * (portion * head_dim), head_dim), portion * head_dim),
            ],
            query_v,
            in_sem.at[2],
        ),
        pltpu.make_async_copy(gain, gain_v, in_sem.at[3]),
    ]
    heads = [lax.rem(own_head + 1 + j, kv_heads) for j in range(kv_heads)]
    weight_loads = [
        pltpu.make_async_copy(weight.at[:, columns(head)], weight_v.at[j], weight_sem.at[j])
        for j, head in enumerate(heads)
    ]
    int_loads = [
        pltpu.make_async_copy(source, target, int_sem.at[n])
        for n, (source, target) in enumerate(
            [
                (table_h, table),
                (slot_h, mig_slot),
                (dest_h, mig_dest),
                (local_h, mig_local),
                (length_h, length),
            ]
        )
    ]
    loads[0].start()
    for load in int_loads:
        load.start()
    loads[1].start()
    loads[2].start()
    loads[3].start()
    for load in weight_loads:
        load.start()

    for load in int_loads:
        load.wait()
    loads[0].wait()
    for r in range(requests):
        stage[r] = pool_v[table[r]]

    def take_leaving(k):
        to_inst = jnp.where(k < inst, k, k + 1)
        slot = mig_slot[0]
        for u in range(1, migrants):
            slot = jnp.where(mig_dest[u, inst] == to_inst, mig_slot[u], slot)
        leaving[k] = pool_v[slot]

    loop(n_inst - 1, take_leaving)

    def page_copy(k):
        to = lax.rem(mp + 1 + k, n_mp)
        return pltpu.make_async_remote_copy(
            src_ref=stage.at[:, :, columns(to // share)],
            dst_ref=cache.at[pl.ds(0, requests), mp],
            send_sem=page_send.at[k],
            recv_sem=page_recv.at[k],
            device_id={"inst": inst, "mp": to},
            device_id_type=MESH,
        )

    def move_copy(way, far, to):
        target = inst + (1 + far) * (1 - 2 * way)
        place = target - 1 + way
        here = inst - way
        return pltpu.make_async_remote_copy(
            src_ref=leaving.at[place, :, columns(to // share)],
            dst_ref=arrived.at[here, mp],
            send_sem=move_send.at[place, to],
            recv_sem=move_recv.at[here, mp],
            device_id={"inst": target, "mp": to},
            device_id_type=MESH,
        )

    def move_wait(k, column):
        pltpu.make_async_remote_copy(
            src_ref=leaving.at[k, :, columns(0)],
            dst_ref=arrived.at[k, column],
            send_sem=move_send.at[k, column],
            recv_sem=move_recv.at[k, column],
            device_id={"inst": jnp.where(k < inst, k, k + 1), "mp": column},
            device_id_type=MESH,
        ).wait_recv()

    def line(way):
        return inst if way == 0 else n_inst - 1 - inst

    def tell(way, far):
        @pl.when((line(way) > 0) & (line(way) + far <= n_inst - 1))
        def _():
            pl.semaphore_signal(
                news.at[way, far],
                inc=1,
                device_id={"inst": inst - 1 + 2 * way, "mp": mp},
                device_id_type=MESH,
            )

    def hear(far, ways):
        for way in ways:

            @pl.when(line(way) + 1 + far <= n_inst - 1)
            def _():
                pl.semaphore_wait(news.at[way, far], 1)

            if far + 1 <= n_inst - 2:
                tell(way, far + 1)

            @pl.when(line(way) + 1 + far <= n_inst - 1)
            def _():
                loop(n_mp, lambda to: move_copy(way, far, to).start())

    def part_copy(j, k):
        to = lax.rem(mp + 1 + k, n_mp)
        return pltpu.make_async_remote_copy(
            src_ref=part_out.at[j],
            dst_ref=part_in.at[k],
            send_sem=part_send.at[k],
            recv_sem=part_recv.at[k],
            device_id={"inst": inst, "mp": to},
            device_id_type=MESH,
        )

    own_copies = [
        pltpu.make_async_copy(
            stage.at[:, :, columns(own_head)], cache.at[pl.ds(0, requests), mp], own_sem.at[0]
        ),
    ]
    for copy in own_copies:
        copy.start()

    count = jnp.int32(0)
    place = [jnp.int32(0)] * migrants
    guest = [jnp.int32(-1)] * migrants
    for k in range(n_inst - 1):
        source = jnp.where(k < inst, k, k + 1)
        for u in range(migrants):
            here = mig_dest[u, source] == inst
            for v in range(migrants):
                hit = here & (count == v)
                place[v] = jnp.where(hit, k, place[v])
                guest[v] = jnp.where(hit, mig_local[u, source], guest[v])
            count = count + jnp.where(here, 1, 0)

    row8 = lax.broadcasted_iota(jnp.int32, (requests, head_dim), 0)
    length8 = jnp.zeros((requests, head_dim), jnp.int32)
    for r in range(requests):
        length8 = jnp.where(row8 == r, length[r], length8)

    half = head_dim // 2
    lane = lax.broadcasted_iota(jnp.int32, (rows, head_dim), 1)
    pair_index = jnp.where(lane < half, lane, lane - half)
    frequency = jnp.exp(-(2.0 * pair_index.astype(F32) / head_dim) * math.log(1000000.0))
    position = jnp.concatenate([(length8 + t).astype(F32) for t in range(steps)], axis=0)
    angle = position * frequency
    cosine = jnp.cos(angle)
    sine = jnp.sin(angle)
    sine = jnp.where(lane < half, -sine, sine)

    stay8 = length8
    for v in range(migrants):
        stay8 = jnp.where(row8 == guest[v], 0, stay8)
    cached_lane = lax.broadcasted_iota(jnp.int32, (requests, requests * context), 1)
    first = lax.broadcasted_iota(jnp.int32, (requests, requests * context), 0) * context
    last = first + jnp.broadcast_to(stay8[:, :1], first.shape)
    bias = jnp.where((cached_lane >= first) & (cached_lane < last), 0.0, -1e30).astype(F32)

    guests = migrants * context
    guest_lane = lax.broadcasted_iota(jnp.int32, (requests, guests), 1)
    guest_row = lax.broadcasted_iota(jnp.int32, (requests, guests), 0)
    guest_length = jnp.broadcast_to(length8[:, :1], guest_lane.shape)
    known = guest_row < 0
    for v in range(migrants):
        known = known | (
            (guest_row == guest[v])
            & (guest_lane >= v * context)
            & (guest_lane < v * context + guest_length)
        )
    guest_bias = jnp.where(known, 0.0, -1e30).astype(F32)
    row = lax.broadcasted_iota(jnp.int32, (rows, 128), 0)
    column = lax.broadcasted_iota(jnp.int32, (rows, 128), 1)
    fresh_bias = jnp.where(
        (lax.rem(row, requests) == lax.rem(column, requests)) & (column <= row), 0.0, -1e30
    ).astype(F32)
    loads[2].wait()
    query = jnp.concatenate(
        [
            query_v[t, :, g * head_dim : (g + 1) * head_dim].astype(F32)
            for g in range(portion)
            for t in range(steps)
        ],
        axis=0,
    ).astype(BF16)
    pl.semaphore_wait(barrier, greetings)
    for way in range(2):
        tell(way, 0)
    loop(n_mp - 1, lambda k: page_copy(k).start())
    for far in range(n_inst - 1):
        hear(far, (1,))

    loads[1].wait()
    features = hidden_v[...].astype(F32).reshape(rows, hidden.shape[2]).astype(BF16)
    for j in range(kv_heads):
        weight_loads[j].wait()
        part_out[j] = dot(features, weight_v[j])
        if share == 1:
            if j < kv_heads - 1:
                part_copy(j, j).start()
        if j < n_inst - 1:
            hear(j, (0,))
    if share > 1:

        def send_part(k):
            to = lax.rem(mp + 1 + k, n_mp)
            j = lax.rem(to // share - own_head - 1 + 2 * kv_heads, kv_heads)
            part_copy(j, k).start()

        loop(n_mp - 1, send_part)

    scale = 1.0 / math.sqrt(head_dim)

    def with_ones(values):
        return jnp.concatenate([values, jnp.ones(values.shape, BF16)], axis=1)

    for far in range(min(kv_heads, n_inst - 1), n_inst - 1):
        hear(far, (0,))

    own_copies[0].wait()
    loop(n_mp - 1, lambda k: page_copy(k).wait_recv())
    held = cache[...].reshape(requests * context, pair)
    total_rows = portion * rows
    scores = dot(query, held[:, :head_dim], ((1,), (1,))) * scale
    scores = scores.reshape(portion * steps, requests, requests * context) + bias[None]
    scores = scores.reshape(total_rows, requests * context)
    peak = jnp.max(scores, axis=-1, keepdims=True)
    summed = weighted(jnp.exp(scores - peak), with_ones(held[:, head_dim:]))

    loads[3].wait()
    loop(n_mp - 1, lambda k: part_copy(0, k).wait_recv())
    projected = part_out[kv_heads - 1]
    for k in range(n_mp - 1):
        projected = projected + part_in[k]
    keys = projected[:, :head_dim]
    factor = lax.rsqrt(jnp.mean(keys * keys, axis=-1, keepdims=True) + 1e-06)
    keys = keys * factor * gain_v[...]
    keys = keys * cosine + pltpu.roll(keys, half, 1) * sine
    blank = jnp.zeros((128 - rows, head_dim), F32)
    fresh_keys = jnp.concatenate([keys, blank], axis=0).astype(BF16)
    fresh_values = jnp.concatenate([projected[:, head_dim:], blank], axis=0).astype(BF16)

    fresh = dot(query, fresh_keys, ((1,), (1,))) * scale
    fresh = (fresh.reshape(portion, rows, 128) + fresh_bias[None]).reshape(total_rows, 128)
    highest = jnp.maximum(peak, jnp.max(fresh, axis=-1, keepdims=True))
    summed = summed * jnp.exp(peak - highest) + weighted(
        jnp.exp(fresh - highest), with_ones(fresh_values)
    )

    loop(n_inst - 1, lambda k: loop(n_mp, lambda column: move_wait(k, column)))
    came = jnp.concatenate(
        [arrived[place[v]].reshape(context, pair) for v in range(migrants)], axis=0
    )
    late = dot(query, came[:, :head_dim], ((1,), (1,))) * scale
    late = late.reshape(portion * steps, requests, guests) + guest_bias[None]
    late = late.reshape(total_rows, guests)
    peak = highest
    highest = jnp.maximum(peak, jnp.max(late, axis=-1, keepdims=True))
    summed = summed * jnp.exp(peak - highest) + weighted(
        jnp.exp(late - highest), with_ones(came[:, head_dim:])
    )
    result = summed[:, :head_dim] / summed[:, head_dim:]
    for t in range(steps):
        for g in range(portion):
            at = (g * steps + t) * requests
            out[t, :, g * head_dim : (g + 1) * head_dim] = result[at : at + requests].astype(BF16)

    loop(n_mp - 1, lambda k: page_copy(k).wait_send())
    for far in range(n_inst - 1):
        for way in range(2):

            @pl.when(line(way) + 1 + far <= n_inst - 1)
            def _():
                loop(n_mp, lambda to: move_copy(way, far, to).wait_send())

    loop(n_mp - 1, lambda k: part_copy(0, k).wait_send())


def local(
    n_inst,
    n_mp,
    hidden_states,
    kv_weight,
    key_gain,
    queries,
    kv_pool,
    page_table,
    lengths,
    mig_dest,
    mig_local,
    mig_slots,
):
    steps, requests, depth = hidden_states.shape
    head_dim = key_gain.shape[0]
    width = kv_weight.shape[1]
    pair = 2 * head_dim
    kv_heads = width // pair
    portion = queries.shape[2] // n_mp
    migrants = mig_dest.shape[1]
    pool = kv_pool[0]
    page = pool.shape[1]
    rows = steps * requests
    assert page_table.shape[1] == 1 and n_mp % kv_heads == 0
    far = pl.BlockSpec(memory_space=pltpu.HBM)
    return pl.pallas_call(
        functools.partial(kernel, n_inst, n_mp, migrants, kv_heads),
        out_shape=jax.ShapeDtypeStruct((steps, requests, portion), BF16),
        in_specs=[far] * 10,
        out_specs=pl.BlockSpec(memory_space=pltpu.VMEM),
        scratch_shapes=[
            pltpu.VMEM(pool.shape, BF16),
            pltpu.VMEM(hidden_states.shape, BF16),
            pltpu.VMEM((kv_heads, depth, pair), BF16),
            pltpu.VMEM((1, head_dim), F32),
            pltpu.VMEM((steps, requests, portion), BF16),
            pltpu.VMEM((requests, page, width), BF16),
            pltpu.VMEM((n_inst - 1, page, width), BF16),
            pltpu.VMEM((requests, n_mp, page, pair), BF16),
            pltpu.VMEM((n_inst - 1, n_mp, page, pair), BF16),
            pltpu.VMEM((kv_heads, rows, pair), F32),
            pltpu.VMEM((n_mp - 1, rows, pair), F32),
            pltpu.SMEM((requests,), jnp.int32),
            pltpu.SMEM((requests,), jnp.int32),
            pltpu.SMEM((migrants, n_inst), jnp.int32),
            pltpu.SMEM((migrants, n_inst), jnp.int32),
            pltpu.SMEM((migrants,), jnp.int32),
            pltpu.SemaphoreType.DMA((5,)),
            pltpu.SemaphoreType.DMA((4,)),
            pltpu.SemaphoreType.DMA((kv_heads,)),
            pltpu.SemaphoreType.DMA((2,)),
            pltpu.SemaphoreType.DMA((n_mp - 1,)),
            pltpu.SemaphoreType.DMA((n_mp - 1,)),
            pltpu.SemaphoreType.DMA((n_inst - 1, n_mp)),
            pltpu.SemaphoreType.DMA((n_inst - 1, n_mp)),
            pltpu.SemaphoreType.REGULAR((2, n_inst)),
            pltpu.SemaphoreType.DMA((n_mp - 1,)),
            pltpu.SemaphoreType.DMA((n_mp - 1,)),
        ],
        compiler_params=pltpu.CompilerParams(
            collective_id=0, has_side_effects=True, vmem_limit_bytes=32 * 1024 * 1024
        ),
    )(
        *[
            pltpu.with_memory_space_constraint(operand, pltpu.HBM)
            for operand in (
                page_table.reshape(-1),
                lengths,
                mig_dest.T,
                mig_local.T,
                mig_slots.reshape(-1),
                hidden_states,
                kv_weight,
                key_gain.reshape(1, head_dim),
                queries,
                pool,
            )
        ]
    )


def solution(mesh):
    placed = (
        P(None, ("groups", "inst"), "mp"),
        P("mp", None),
        P(),
        P(None, ("groups", "inst"), None),
        P(("groups", "inst"), "mp", None, None),
        P(("groups", "inst"), None, "mp"),
        P(("groups", "inst")),
        P("groups", None),
        P("groups", None),
        P(("groups", "inst"), None, None, "mp"),
    )
    return jax.shard_map(
        functools.partial(local, mesh.shape["inst"], mesh.shape["mp"]),
        mesh=mesh,
        in_specs=placed,
        out_specs=P(None, ("groups", "inst"), "mp"),
        check_vma=False,
    )
```

```python
import functools
import math

import jax
import jax.numpy as jnp
from jax import lax
from jax.experimental import pallas as pl
from jax.experimental.pallas import tpu as pltpu
from jax.sharding import PartitionSpec as P

MESH = pl.DeviceIdType.MESH
F32 = jnp.float32
BF16 = jnp.bfloat16


def loop(count, step):
    if count <= 4:
        for index in range(count):
            step(index)
    else:
        lax.fori_loop(0, count, lambda index, carry: (step(index), carry)[1], 0)


def dot(left, right, contract=((1,), (0,))):
    return lax.dot_general(left, right, (contract, ((), ())), preferred_element_type=F32)


def weighted(weights, values):
    high = weights.astype(BF16)
    low = (weights - high.astype(F32)).astype(BF16)
    return dot(high, values) + dot(low, values)


def kernel(
    n_inst,
    n_mp,
    migrants,
    kv_heads,
    table_h,
    length_h,
    dest_h,
    local_h,
    slot_h,
    hidden,
    weight,
    gain,
    queries,
    pool,
    out,
    pool_v,
    hidden_v,
    weight_v,
    gain_v,
    query_v,
    stage,
    leaving,
    cache,
    arrived,
    part_out,
    part_in,
    table,
    length,
    mig_dest,
    mig_local,
    mig_slot,
    int_sem,
    in_sem,
    weight_sem,
    own_sem,
    page_send,
    page_recv,
    move_send,
    move_recv,
    news,
    part_send,
    part_recv,
):
    inst = lax.axis_index("inst")
    mp = lax.axis_index("mp")
    steps, requests, _ = hidden.shape
    head_dim = gain.shape[1]
    pair = 2 * head_dim
    page = pool.shape[1]
    rows = steps * requests
    portion = query_v.shape[2] // head_dim
    share = n_mp // kv_heads
    context = n_mp * page
    own_head = mp // share

    def columns(head):
        return pl.ds(pl.multiple_of(head * pair, pair), pair)

    barrier = pltpu.get_barrier_semaphore()

    def greet_peer(k):
        pl.semaphore_signal(
            barrier,
            inc=1,
            device_id={"inst": inst, "mp": lax.rem(mp + 1 + k, n_mp)},
            device_id_type=MESH,
        )

    loop(n_mp - 1, greet_peer)
    for away, there in ((1, inst < n_inst - 1), (-1, inst > 0)):

        @pl.when(there)
        def _():
            pl.semaphore_signal(
                barrier, inc=1, device_id={"inst": inst + away, "mp": mp}, device_id_type=MESH
            )

    greetings = (
        n_mp - 1 + jnp.where(inst < n_inst - 1, 1, 0) + jnp.where(inst > 0, 1, 0)
    )

    loads = [
        pltpu.make_async_copy(pool, pool_v, in_sem.at[0]),
        pltpu.make_async_copy(hidden, hidden_v, in_sem.at[1]),
        pltpu.make_async_copy(
            queries.at[
                :,
                :,
                pl.ds(pl.multiple_of(mp * (portion * head_dim), head_dim), portion * head_dim),
            ],
            query_v,
            in_sem.at[2],
        ),
        pltpu.make_async_copy(gain, gain_v, in_sem.at[3]),
    ]
    heads = [lax.rem(own_head + 1 + j, kv_heads) for j in range(kv_heads)]
    weight_loads = [
        pltpu.make_async_copy(weight.at[:, columns(head)], weight_v.at[j], weight_sem.at[j])
        for j, head in enumerate(heads)
    ]
    int_loads = [
        pltpu.make_async_copy(source, target, int_sem.at[n])
        for n, (source, target) in enumerate(
            [
                (table_h, table),
                (slot_h, mig_slot),
                (dest_h, mig_dest),
                (local_h, mig_local),
                (length_h, length),
            ]
        )
    ]
    loads[0].start()
    for load in int_loads:
        load.start()
    loads[1].start()
    loads[2].start()
    loads[3].start()
    for load in weight_loads:
        load.start()

    for load in int_loads:
        load.wait()
    loads[0].wait()
    for r in range(requests):
        stage[r] = pool_v[table[r]]

    def take_leaving(k):
        to_inst = jnp.where(k < inst, k, k + 1)
        slot = mig_slot[0]
        for u in range(1, migrants):
            slot = jnp.where(mig_dest[u, inst] == to_inst, mig_slot[u], slot)
        leaving[k] = pool_v[slot]

    loop(n_inst - 1, take_leaving)

    def page_copy(k):
        to = lax.rem(mp + 1 + k, n_mp)
        return pltpu.make_async_remote_copy(
            src_ref=stage.at[:, :, columns(to // share)],
            dst_ref=cache.at[pl.ds(0, requests), mp],
            send_sem=page_send.at[k],
            recv_sem=page_recv.at[k],
            device_id={"inst": inst, "mp": to},
            device_id_type=MESH,
        )

    def move_copy(way, far, to):
        target = inst + (1 + far) * (1 - 2 * way)
        place = target - 1 + way
        here = inst - way
        return pltpu.make_async_remote_copy(
            src_ref=leaving.at[place, :, columns(to // share)],
            dst_ref=arrived.at[here, mp],
            send_sem=move_send.at[place, to],
            recv_sem=move_recv.at[here, mp],
            device_id={"inst": target, "mp": to},
            device_id_type=MESH,
        )

    def move_wait(k, column):
        pltpu.make_async_remote_copy(
            src_ref=leaving.at[k, :, columns(0)],
            dst_ref=arrived.at[k, column],
            send_sem=move_send.at[k, column],
            recv_sem=move_recv.at[k, column],
            device_id={"inst": jnp.where(k < inst, k, k + 1), "mp": column},
            device_id_type=MESH,
        ).wait_recv()

    def line(way):
        return inst if way == 0 else n_inst - 1 - inst

    def tell(way, far):
        @pl.when((line(way) > 0) & (line(way) + far <= n_inst - 1))
        def _():
            pl.semaphore_signal(
                news.at[way, far],
                inc=1,
                device_id={"inst": inst - 1 + 2 * way, "mp": mp},
                device_id_type=MESH,
            )

    def hear(far, ways):
        for way in ways:

            @pl.when(line(way) + 1 + far <= n_inst - 1)
            def _():
                pl.semaphore_wait(news.at[way, far], 1)

            if far + 1 <= n_inst - 2:
                tell(way, far + 1)

            @pl.when(line(way) + 1 + far <= n_inst - 1)
            def _():
                loop(n_mp, lambda to: move_copy(way, far, to).start())

    def part_copy(j, k):
        to = lax.rem(mp + 1 + k, n_mp)
        return pltpu.make_async_remote_copy(
            src_ref=part_out.at[j],
            dst_ref=part_in.at[k],
            send_sem=part_send.at[k],
            recv_sem=part_recv.at[k],
            device_id={"inst": inst, "mp": to},
            device_id_type=MESH,
        )

    own_copies = [
        pltpu.make_async_copy(
            stage.at[:, :, columns(own_head)], cache.at[pl.ds(0, requests), mp], own_sem.at[0]
        ),
    ]
    for copy in own_copies:
        copy.start()

    count = jnp.int32(0)
    place = [jnp.int32(0)] * migrants
    guest = [jnp.int32(-1)] * migrants
    for k in range(n_inst - 1):
        source = jnp.where(k < inst, k, k + 1)
        for u in range(migrants):
            here = mig_dest[u, source] == inst
            for v in range(migrants):
                hit = here & (count == v)
                place[v] = jnp.where(hit, k, place[v])
                guest[v] = jnp.where(hit, mig_local[u, source], guest[v])
            count = count + jnp.where(here, 1, 0)

    row8 = lax.broadcasted_iota(jnp.int32, (requests, head_dim), 0)
    length8 = jnp.zeros((requests, head_dim), jnp.int32)
    for r in range(requests):
        length8 = jnp.where(row8 == r, length[r], length8)

    half = head_dim // 2
    lane = lax.broadcasted_iota(jnp.int32, (rows, head_dim), 1)
    pair_index = jnp.where(lane < half, lane, lane - half)
    frequency = jnp.exp(-(2.0 * pair_index.astype(F32) / head_dim) * math.log(1000000.0))
    position = jnp.concatenate([(length8 + t).astype(F32) for t in range(steps)], axis=0)
    angle = position * frequency
    cosine = jnp.cos(angle)
    sine = jnp.sin(angle)
    sine = jnp.where(lane < half, -sine, sine)

    stay8 = length8
    for v in range(migrants):
        stay8 = jnp.where(row8 == guest[v], 0, stay8)
    cached_lane = lax.broadcasted_iota(jnp.int32, (requests, requests * context), 1)
    first = lax.broadcasted_iota(jnp.int32, (requests, requests * context), 0) * context
    last = first + jnp.broadcast_to(stay8[:, :1], first.shape)
    bias = jnp.where((cached_lane >= first) & (cached_lane < last), 0.0, -1e30).astype(F32)

    guests = migrants * context
    guest_lane = lax.broadcasted_iota(jnp.int32, (requests, guests), 1)
    guest_row = lax.broadcasted_iota(jnp.int32, (requests, guests), 0)
    guest_length = jnp.broadcast_to(length8[:, :1], guest_lane.shape)
    known = guest_row < 0
    for v in range(migrants):
        known = known | (
            (guest_row == guest[v])
            & (guest_lane >= v * context)
            & (guest_lane < v * context + guest_length)
        )
    guest_bias = jnp.where(known, 0.0, -1e30).astype(F32)
    row = lax.broadcasted_iota(jnp.int32, (rows, 128), 0)
    column = lax.broadcasted_iota(jnp.int32, (rows, 128), 1)
    fresh_bias = jnp.where(
        (lax.rem(row, requests) == lax.rem(column, requests)) & (column <= row), 0.0, -1e30
    ).astype(F32)
    loads[2].wait()
    query = jnp.concatenate(
        [
            query_v[t, :, g * head_dim : (g + 1) * head_dim].astype(F32)
            for g in range(portion)
            for t in range(steps)
        ],
        axis=0,
    ).astype(BF16)
    pl.semaphore_wait(barrier, greetings)
    for way in range(2):
        tell(way, 0)
    for far in range(n_inst - 1):
        hear(far, (1,))
    loop(n_mp - 1, lambda k: page_copy(k).start())

    loads[1].wait()
    features = hidden_v[...].astype(F32).reshape(rows, hidden.shape[2]).astype(BF16)
    for j in range(kv_heads):
        weight_loads[j].wait()
        part_out[j] = dot(features, weight_v[j])
        if share == 1:
            if j < kv_heads - 1:
                part_copy(j, j).start()
        if j < n_inst - 1:
            hear(j, (0,))
    if share > 1:

        def send_part(k):
            to = lax.rem(mp + 1 + k, n_mp)
            j = lax.rem(to // share - own_head - 1 + 2 * kv_heads, kv_heads)
            part_copy(j, k).start()

        loop(n_mp - 1, send_part)

    scale = 1.0 / math.sqrt(head_dim)

    def with_ones(values):
        return jnp.concatenate([values, jnp.ones(values.shape, BF16)], axis=1)

    for far in range(min(kv_heads, n_inst - 1), n_inst - 1):
        hear(far, (0,))

    own_copies[0].wait()
    loop(n_mp - 1, lambda k: page_copy(k).wait_recv())
    held = cache[...].reshape(requests * context, pair)
    total_rows = portion * rows
    scores = dot(query, held[:, :head_dim], ((1,), (1,))) * scale
    scores = scores.reshape(portion * steps, requests, requests * context) + bias[None]
    scores = scores.reshape(total_rows, requests * context)
    peak = jnp.max(scores, axis=-1, keepdims=True)
    summed = weighted(jnp.exp(scores - peak), with_ones(held[:, head_dim:]))

    loads[3].wait()
    loop(n_mp - 1, lambda k: part_copy(0, k).wait_recv())
    projected = part_out[kv_heads - 1]
    for k in range(n_mp - 1):
        projected = projected + part_in[k]
    keys = projected[:, :head_dim]
    factor = lax.rsqrt(jnp.mean(keys * keys, axis=-1, keepdims=True) + 1e-06)
    keys = keys * factor * gain_v[...]
    keys = keys * cosine + pltpu.roll(keys, half, 1) * sine
    blank = jnp.zeros((128 - rows, head_dim), F32)
    fresh_keys = jnp.concatenate([keys, blank], axis=0).astype(BF16)
    fresh_values = jnp.concatenate([projected[:, head_dim:], blank], axis=0).astype(BF16)

    fresh = dot(query, fresh_keys, ((1,), (1,))) * scale
    fresh = (fresh.reshape(portion, rows, 128) + fresh_bias[None]).reshape(total_rows, 128)
    highest = jnp.maximum(peak, jnp.max(fresh, axis=-1, keepdims=True))
    summed = summed * jnp.exp(peak - highest) + weighted(
        jnp.exp(fresh - highest), with_ones(fresh_values)
    )

    loop(n_inst - 1, lambda k: loop(n_mp, lambda column: move_wait(k, column)))
    came = jnp.concatenate(
        [arrived[place[v]].reshape(context, pair) for v in range(migrants)], axis=0
    )
    late = dot(query, came[:, :head_dim], ((1,), (1,))) * scale
    late = late.reshape(portion * steps, requests, guests) + guest_bias[None]
    late = late.reshape(total_rows, guests)
    peak = highest
    highest = jnp.maximum(peak, jnp.max(late, axis=-1, keepdims=True))
    summed = summed * jnp.exp(peak - highest) + weighted(
        jnp.exp(late - highest), with_ones(came[:, head_dim:])
    )
    result = summed[:, :head_dim] / summed[:, head_dim:]
    for t in range(steps):
        for g in range(portion):
            at = (g * steps + t) * requests
            out[t, :, g * head_dim : (g + 1) * head_dim] = result[at : at + requests].astype(BF16)

    loop(n_mp - 1, lambda k: page_copy(k).wait_send())
    for far in range(n_inst - 1):
        for way in range(2):

            @pl.when(line(way) + 1 + far <= n_inst - 1)
            def _():
                loop(n_mp, lambda to: move_copy(way, far, to).wait_send())

    loop(n_mp - 1, lambda k: part_copy(0, k).wait_send())


def local(
    n_inst,
    n_mp,
    hidden_states,
    kv_weight,
    key_gain,
    queries,
    kv_pool,
    page_table,
    lengths,
    mig_dest,
    mig_local,
    mig_slots,
):
    steps, requests, depth = hidden_states.shape
    head_dim = key_gain.shape[0]
    width = kv_weight.shape[1]
    pair = 2 * head_dim
    kv_heads = width // pair
    portion = queries.shape[2] // n_mp
    migrants = mig_dest.shape[1]
    pool = kv_pool[0]
    page = pool.shape[1]
    rows = steps * requests
    assert page_table.shape[1] == 1 and n_mp % kv_heads == 0
    far = pl.BlockSpec(memory_space=pltpu.HBM)
    return pl.pallas_call(
        functools.partial(kernel, n_inst, n_mp, migrants, kv_heads),
        out_shape=jax.ShapeDtypeStruct((steps, requests, portion), BF16),
        in_specs=[far] * 10,
        out_specs=pl.BlockSpec(memory_space=pltpu.VMEM),
        scratch_shapes=[
            pltpu.VMEM(pool.shape, BF16),
            pltpu.VMEM(hidden_states.shape, BF16),
            pltpu.VMEM((kv_heads, depth, pair), BF16),
            pltpu.VMEM((1, head_dim), F32),
            pltpu.VMEM((steps, requests, portion), BF16),
            pltpu.VMEM((requests, page, width), BF16),
            pltpu.VMEM((n_inst - 1, page, width), BF16),
            pltpu.VMEM((requests, n_mp, page, pair), BF16),
            pltpu.VMEM((n_inst - 1, n_mp, page, pair), BF16),
            pltpu.VMEM((kv_heads, rows, pair), F32),
            pltpu.VMEM((n_mp - 1, rows, pair), F32),
            pltpu.SMEM((requests,), jnp.int32),
            pltpu.SMEM((requests,), jnp.int32),
            pltpu.SMEM((migrants, n_inst), jnp.int32),
            pltpu.SMEM((migrants, n_inst), jnp.int32),
            pltpu.SMEM((migrants,), jnp.int32),
            pltpu.SemaphoreType.DMA((5,)),
            pltpu.SemaphoreType.DMA((4,)),
            pltpu.SemaphoreType.DMA((kv_heads,)),
            pltpu.SemaphoreType.DMA((2,)),
            pltpu.SemaphoreType.DMA((n_mp - 1,)),
            pltpu.SemaphoreType.DMA((n_mp - 1,)),
            pltpu.SemaphoreType.DMA((n_inst - 1, n_mp)),
            pltpu.SemaphoreType.DMA((n_inst - 1, n_mp)),
            pltpu.SemaphoreType.REGULAR((2, n_inst)),
            pltpu.SemaphoreType.DMA((n_mp - 1,)),
            pltpu.SemaphoreType.DMA((n_mp - 1,)),
        ],
        compiler_params=pltpu.CompilerParams(
            collective_id=0, has_side_effects=True, vmem_limit_bytes=32 * 1024 * 1024
        ),
    )(
        *[
            pltpu.with_memory_space_constraint(operand, pltpu.HBM)
            for operand in (
                page_table.reshape(-1),
                lengths,
                mig_dest.T,
                mig_local.T,
                mig_slots.reshape(-1),
                hidden_states,
                kv_weight,
                key_gain.reshape(1, head_dim),
                queries,
                pool,
            )
        ]
    )


def solution(mesh):
    placed = (
        P(None, ("groups", "inst"), "mp"),
        P("mp", None),
        P(),
        P(None, ("groups", "inst"), None),
        P(("groups", "inst"), "mp", None, None),
        P(("groups", "inst"), None, "mp"),
        P(("groups", "inst")),
        P("groups", None),
        P("groups", None),
        P(("groups", "inst"), None, None, "mp"),
    )
    return jax.shard_map(
        functools.partial(local, mesh.shape["inst"], mesh.shape["mp"]),
        mesh=mesh,
        in_specs=placed,
        out_specs=P(None, ("groups", "inst"), "mp"),
        check_vma=False,
    )
```
